512 devices in a mesh: row: 32 (over x, z_lo, core), col: 16 (over y, z_hi).
Axes of the slice: x: 4, y: 4, z: 16 (z_hi: 4, z_lo: 4; z = z_hi * 4 + z_lo), core: 2. Of those that a mesh axis runs over, the one named last changes fastest.
Arguments:
- site_tensor: bfloat16 [4096, 2, 4096], P('row', None, 'col'), may hold values from -6 to 6
- left_env: bfloat16 [16, 4096, 4096], P(None, 'row', 'col'), may hold values from -0.0234375 to 0.0234375
- right_env: bfloat16 [4096, 16, 768], P('row', None, 'col'), may hold values from -0.09375 to 0.09375
- mpo_out: int32 [48], replicated, may hold values from 0 to 15
- mpo_in: int32 [48], replicated, may hold values from 0 to 15
- mpo_ops: bfloat16 [48, 2, 2], replicated, may hold values from -3 to 3
Outputs:
- gradient: bfloat16 [4096, 2, 768], P('col', None, 'row')
The draws below stay inside these ranges and needn't reach their ends.
All inputs are finite; a program needn't handle non-finite values.
Results may differ from the reference program's by a relative error of at most 0.0059.
Values may be sent and summed in bfloat16 or wider, within the bound.
A program may use at most 64 MiB of HBM per device.

```python
import jax
import jax.numpy as jnp
from jax import lax

CHI = 4096
PHYS = 2
MPOW = 16
NNZ = 48
SLAB = 768


def set_ends(result, key, low, high):
    longest = result.shape.index(max(result.shape))
    spots = []
    for shift in (0, 1):
        where = [jax.random.randint(jax.random.fold_in(key, axis), (), 0, length) for axis, length in enumerate(result.shape)]
        where[longest] = (where[longest] + shift) % result.shape[longest]
        spots.append(tuple(where))
    return result.at[spots[0]].set(low).at[spots[1]].set(high)


def level_of(rng, shape, split, least, high):
    def one(position, shards_of):
        draws = jax.random.uniform(jax.random.fold_in(jax.random.fold_in(rng, 6), position), (shards_of,), jnp.float32, least / len(split), high / len(split))
        return jnp.repeat(jnp.exp(draws), shape[position] // shards_of).reshape((-1,) + (1,) * (len(shape) - position - 1))

    gain = one(*split[0])
    for cut in split[1:]:
        gain = gain * one(*cut)
    return gain


def bell_draw(rng, extent, scale, bound, cuts=(), held_as=jnp.bfloat16):
    loudness = level_of(rng, extent, cuts, -0.22, 0.18) if cuts else 1.0
    values = jax.random.normal(rng, extent, jnp.float32) * scale * loudness
    return jnp.minimum(jnp.maximum(values, -bound), bound).astype(held_as)


def setup_inputs(seed: int = 0) -> dict:
    key_list = jax.random.split(jax.random.key(seed), 7)
    return {
        "site_tensor": bell_draw(key_list[0], (CHI, PHYS, CHI), 1.0, 6.0, ((0, 32), (2, 16))),
        "left_env": bell_draw(key_list[1], (MPOW, CHI, CHI), (MPOW * CHI) ** -0.5, 0.0234375, ((1, 32), (2, 16))),
        "right_env": bell_draw(key_list[2], (CHI, MPOW, SLAB), CHI ** -0.5, 0.09375, ((0, 32), (2, 16))),
        "mpo_out": set_ends(jax.random.randint(key_list[3], (NNZ,), 0, MPOW), jax.random.fold_in(key_list[3], 1), 0, MPOW - 1).astype(jnp.int32),
        "mpo_in": set_ends(jax.random.randint(key_list[4], (NNZ,), 0, MPOW), jax.random.fold_in(key_list[4], 1), 0, MPOW - 1).astype(jnp.int32),
        "mpo_ops": bell_draw(key_list[5], (NNZ, PHYS, PHYS), 0.5, 3.0),
    }


def dense_mpo(mpo_out, mpo_in, mpo_ops):
    channels = jnp.arange(MPOW, dtype=jnp.int32)
    pick_out = (mpo_out[:, None] == channels[None, :]).astype(jnp.float32)
    pick_in = (mpo_in[:, None] == channels[None, :]).astype(jnp.float32)
    dense = jnp.einsum("nw,nv,nst->wsvt", pick_out, pick_in, mpo_ops.astype(jnp.float32), precision=lax.Precision.HIGHEST)
    return dense.astype(jnp.bfloat16)


def reference(site_tensor, left_env, right_env, mpo_out, mpo_in, mpo_ops):
    mpo_dense = lax.optimization_barrier(dense_mpo(mpo_out, mpo_in, mpo_ops))
    mixed_rows = jnp.dot(site_tensor.reshape(CHI * PHYS, CHI), right_env.reshape(CHI, MPOW * SLAB), preferred_element_type=jnp.float32)
    mixed_rows = lax.optimization_barrier(mixed_rows.astype(jnp.bfloat16))
    widened = mixed_rows.reshape(CHI, PHYS, MPOW, SLAB).astype(jnp.float32)
    channel = jnp.einsum("wsvt,xtvb->wxsb", mpo_dense.astype(jnp.float32), widened, precision=lax.Precision.HIGHEST)
    channel = lax.optimization_barrier(channel.astype(jnp.bfloat16))

    def add_channel(running, slices):
        left_slice, channel_slice = slices
        update = jnp.dot(jnp.transpose(left_slice), channel_slice.reshape(CHI, PHYS * SLAB), preferred_element_type=jnp.float32)
        return running + update, None

    initial = jnp.zeros((CHI, PHYS * SLAB), jnp.float32)
    running, leftover = lax.scan(add_channel, initial, (left_env, channel))
    return running.reshape(CHI, PHYS, SLAB).astype(jnp.bfloat16)
```

```python
import jax
import jax.numpy as jnp
from jax import lax
from jax.experimental import pallas as pl
from jax.experimental.pallas import tpu as pltpu
from jax.sharding import PartitionSpec as P

MESH = pl.DeviceIdType.MESH
BF16 = jnp.bfloat16
F32 = jnp.float32

N_COPIES = 128
NX, NZL, NY, NZH = 4, 4, 4, 4


def kernel(
    site_ref, right_ref, left_ref, out_idx_ref, in_idx_ref, ops_ref, result_ref,
    site_all, right_all, chan_all, mixed, expand, keep, to_sibling, from_sibling, to_x, from_x, to_z, from_z,
    send_sems, recv_sems, x_send, x_recv,
):
    r = lax.axis_index("row")
    c = lax.axis_index("col")
    x, zl, k = r // 8, (r // 2) % 4, r % 2
    y, zh = c // 4, c % 4

    def row_of(dx=0, dz=0, dk=0):
        return ((x + dx + 4) % 4) * 8 + ((zl + dz + 4) % 4) * 2 + (k + dk) % 2

    def col_of(dy=0, dz=0):
        return ((y + dy + 4) % 4) * 4 + (zh + dz + 4) % 4

    sibling = (row_of(dk=1), c)
    z_up, z_down = (r, col_of(dz=1)), (r, col_of(dz=-1))
    y_up, y_down = (r, col_of(dy=1)), (r, col_of(dy=-1))
    x_up, x_down, x_far = (row_of(dx=1), c), (row_of(dx=-1), c), (row_of(dx=2), c)
    line = [(row_of(dz=d), c) for d in (1, 2, 3)]

    barrier = pltpu.get_barrier_semaphore()
    partners = [sibling, z_up, z_down, y_up, y_down, x_up, x_down, x_far] + line
    for partner in partners:
        pl.semaphore_signal(barrier, inc=1, device_id=partner, device_id_type=MESH)
    pl.semaphore_wait(barrier, len(partners))

    started = []

    def send(src, dst, device):
        n = len(started)
        copy = pltpu.make_async_remote_copy(
            src_ref=src, dst_ref=dst, send_sem=send_sems.at[n], recv_sem=recv_sems.at[n],
            device_id=device, device_id_type=MESH,
        )
        copy.start()
        started.append(copy)
        return n

    def arrive(n, dst, device):
        pltpu.make_async_remote_copy(
            src_ref=dst, dst_ref=dst, send_sem=send_sems.at[n], recv_sem=recv_sems.at[n],
            device_id=device, device_id_type=MESH,
        ).wait_recv()

    class Ring:
        def __init__(self, at, up, down, low, high, far):
            self.at, self.up, self.down = at, up, down
            self.low, self.high, self.far = low, high, far

        def begin(self, src, own):
            self.n_up = send(src, self.at(own), self.up)
            self.n_down = send(src, self.at(own), self.down)

        def near(self):
            arrive(self.n_up, self.at(self.low), self.down)
            self.n_low = send(self.at(self.low).at[0], self.at(self.low).at[0], self.up)
            arrive(self.n_down, self.at(self.high), self.up)
            self.n_high = send(self.at(self.high).at[1], self.at(self.high).at[1], self.down)

        def end(self):
            arrive(self.n_low, self.at(self.far).at[0], self.down)
            arrive(self.n_high, self.at(self.far).at[1], self.up)

    right_at = lambda origin: right_all.at[origin]
    rights = []

    def to_core(origin, src=None):
        rights_k.append((send(right_at(origin) if src is None else src, right_at(origin), sibling), origin))

    rights_k = []
    line_n = [send(right_ref, right_at(r), peer) for peer in line]
    site_at = lambda origin: site_all.at[origin]
    site_z = Ring(site_at, z_up, z_down, col_of(dz=-1), col_of(dz=1), col_of(dz=2))
    site_z.begin(site_ref, c)

    def x_ring(dz):
        return Ring(right_at, x_up, x_down, row_of(dx=-1, dz=dz), row_of(dx=1, dz=dz), row_of(dx=2, dz=dz))

    def y_ring(at, dz):
        return Ring(at, y_up, y_down, col_of(dy=-1, dz=dz), col_of(dy=1, dz=dz), col_of(dy=2, dz=dz))

    right_x = {0: x_ring(0)}
    right_x[0].begin(right_ref, r)
    site_y = {0: y_ring(site_at, 0)}
    site_y[0].begin(site_ref, c)
    to_core(r, right_ref)

    site_all[c] = site_ref[...]
    right_all[r] = right_ref[...]

    channel_rows = lax.broadcasted_iota(jnp.int32, (16, 48), 0)
    pick_out = channel_rows == jnp.broadcast_to(out_idx_ref[...], (16, 48))
    pick_in = (channel_rows == jnp.broadcast_to(in_idx_ref[...], (16, 48))).astype(F32).astype(BF16)
    spread = (
        lax.broadcasted_iota(jnp.int32, (128, 16), 0) // 8 == lax.broadcasted_iota(jnp.int32, (128, 16), 1)
    ).astype(F32).astype(BF16)
    same = (lax.broadcasted_iota(jnp.int32, (128, 128), 0) % 8) == (lax.broadcasted_iota(jnp.int32, (128, 128), 1) % 8)
    for s in range(2):
        for t in range(2):
            op = ops_ref[pl.ds(2 * s + t, 1), :].astype(F32)
            picked = jnp.where(pick_out, jnp.broadcast_to(op, (16, 48)), 0.0).astype(BF16)
            dense = lax.dot_general(picked, pick_in, (((1,), (1,)), ((), ())), preferred_element_type=F32).astype(BF16)
            tall = jnp.dot(spread, dense, preferred_element_type=F32).astype(BF16)
            wide = lax.dot_general(tall, spread, (((1,), (1,)), ((), ())), preferred_element_type=F32)
            expand[pl.ds(128 * s, 128), pl.ds(128 * t, 128)] = jnp.where(same, wide, 0.0).astype(BF16)

    def x_near(dz):
        right_x[dz].near()
        to_core(right_x[dz].low)
        to_core(right_x[dz].high)

    def x_end(dz):
        right_x[dz].end()
        to_core(right_x[dz].far)

    def line_arrives(d):
        origin = row_of(dz=-d)
        arrive(line_n[d - 1], right_at(origin), line[4 - d - 1])
        right_x[-d] = x_ring(-d)
        right_x[-d].begin(right_at(origin), origin)
        to_core(origin)

    def site_pass(dz):
        site_y[dz] = y_ring(site_at, dz)
        site_y[dz].begin(site_at(col_of(dz=dz)), col_of(dz=dz))

    x_near(0)
    site_y[0].near()
    line_arrives(1)
    line_arrives(3)
    site_z.near()
    site_pass(-1)
    site_pass(1)
    x_end(0)
    site_y[0].end()
    line_arrives(2)
    x_near(-1)
    x_near(-3)
    site_z.end()
    site_pass(2)
    site_y[-1].near()
    site_y[1].near()
    x_end(-1)
    x_end(-3)
    x_near(-2)
    site_y[-1].end()
    site_y[1].end()
    site_y[2].near()
    x_end(-2)
    site_y[2].end()
    for n, origin in rights_k:
        other = origin + 1 - 2 * k
        arrive(n, right_at(other), sibling)

    mixed[...] = jnp.zeros_like(mixed)

    def add_block(block, carry):
        env = jnp.concatenate(
            [right_all[2 * block].reshape(768, 128), right_all[2 * block + 1].reshape(768, 128)], axis=1
        )
        site = site_all[block].reshape(256, 256)
        update = lax.dot_general(env, site, (((1,), (1,)), ((), ())), preferred_element_type=F32)
        mixed[...] += update.reshape(16, 48, 256)
        return carry

    lax.fori_loop(0, 16, add_block, 0)

    def make_channel(half):
        results = []
        for part in range(3):
            run = mixed[:, pl.ds(pl.multiple_of(half * 24 + part * 8, 8), 8), :].reshape(128, 256).astype(BF16)
            stacked = jnp.concatenate([run[:, :128], run[:, 128:]], axis=0)
            results.append(jnp.dot(expand[...], stacked, preferred_element_type=F32))

        def eight(u, h):
            s, part = u // 3, u % 3
            pieces = [results[part][s * 128 + w * 8:s * 128 + w * 8 + 8, :] for w in range(8 * h, 8 * h + 8)]
            return jnp.concatenate(pieces, axis=1)

        for h in range(2):
            for m in range(3):
                rows = jnp.concatenate([eight(2 * m, h), eight(2 * m + 1, h)], axis=0)
                chan_all[c, half, h, pl.ds(16 * m, 16), :] = rows.astype(BF16)

    halves = [1 - k, k]
    chan_at = [lambda origin: chan_all.at[origin, halves[0]], lambda origin: chan_all.at[origin, halves[1]]]
    chan_z, chan_y = [], [{}, {}]

    def chan_pass(i, dz):
        chan_y[i][dz] = y_ring(chan_at[i], dz)
        chan_y[i][dz].begin(chan_at[i](col_of(dz=dz)), col_of(dz=dz))

    for i in range(2):
        make_channel(halves[i])
        ring = Ring(chan_at[i], z_up, z_down, col_of(dz=-1), col_of(dz=1), col_of(dz=2))
        ring.begin(chan_at[i](c), c)
        chan_z.append(ring)
        chan_pass(i, 0)

    def gradient(dy, i):
        group = (y + dy) % 4
        total = None
        for h in range(2):
            lhs = jnp.concatenate([chan_all[group * 4 + j, halves[i], h] for j in range(4)], axis=0)
            term = jnp.dot(lhs, left_ref[pl.ds(1024 * h, 1024), :], preferred_element_type=F32)
            total = term if total is None else total + term
        return total

    sib_n = {}

    def share_other(dy):
        to_sibling[dy] = gradient(dy, 0).astype(BF16)
        sib_n[dy] = send(to_sibling.at[dy], from_sibling.at[dy], sibling)

    def share_own(dy):
        total = gradient(dy, 1)
        arrive(sib_n[dy], from_sibling.at[dy], sibling)
        total = total + from_sibling[dy].astype(F32)
        group = (y + dy) % 4

        @pl.when(group == x)
        def _():
            keep[...] = total

        @pl.when(group != x)
        def _():
            to_x[dy] = total.astype(BF16)
            pltpu.make_async_remote_copy(
                src_ref=to_x.at[dy], dst_ref=from_x.at[x], send_sem=x_send.at[dy], recv_sem=x_recv.at[x],
                device_id=(group * 8 + zl * 2 + k, c), device_id_type=MESH,
            ).start()

    chan_y[0][0].near()
    chan_y[1][0].near()
    chan_y[0][0].end()
    chan_z[0].near()
    chan_pass(0, -1)
    chan_pass(0, 1)
    chan_y[1][0].end()
    chan_z[1].near()
    chan_pass(1, -1)
    chan_pass(1, 1)
    chan_z[0].end()
    chan_pass(0, 2)
    chan_y[0][-1].near()
    chan_y[0][1].near()
    share_other(0)
    chan_z[1].end()
    chan_pass(1, 2)
    chan_y[1][-1].near()
    chan_y[1][1].near()
    share_own(0)
    chan_y[0][-1].end()
    chan_y[0][1].end()
    chan_y[0][2].near()
    share_other(1)
    share_other(3)
    chan_y[1][-1].end()
    chan_y[1][1].end()
    chan_y[1][2].near()
    share_own(1)
    share_own(3)
    chan_y[0][2].end()
    share_other(2)
    chan_y[1][2].end()
    share_own(2)

    total = keep[...]
    for d in (1, 3, 2):
        origin = (x + d) % 4
        pltpu.make_async_remote_copy(
            src_ref=from_x.at[origin], dst_ref=from_x.at[origin], send_sem=x_send.at[0], recv_sem=x_recv.at[origin],
            device_id=(row_of(dx=d), c), device_id_type=MESH,
        ).wait_recv()
        total = total + from_x[origin].astype(F32)
    keep[...] = total
    for j in range(4):
        to_z[j] = total[j * 48:(j + 1) * 48, :].astype(BF16)
    z_n = [send(to_z.at[(zl + d) % 4], from_z.at[zl], line[d - 1]) for d in (1, 2, 3)]
    final = keep[pl.ds(pl.multiple_of(zl * 48, 48), 48), :]
    for d in (1, 2, 3):
        origin = (zl - d + 4) % 4
        arrive(z_n[d - 1], from_z.at[origin], line[4 - d - 1])
        final = final + from_z[origin].astype(F32)
    result_ref[...] = final.reshape(2, 24, 256).astype(BF16)

    for copy in started:
        copy.wait_send()
    for dy in range(4):
        group = (y + dy) % 4

        @pl.when(group != x)
        def _():
            pltpu.make_async_remote_copy(
                src_ref=to_x.at[dy], dst_ref=from_x.at[x], send_sem=x_send.at[dy], recv_sem=x_recv.at[x],
                device_id=(group * 8 + zl * 2 + k, c), device_id_type=MESH,
            ).wait_send()


def local(site_tensor, left_env, right_env, mpo_out, mpo_in, mpo_ops):
    site = jnp.transpose(site_tensor, (1, 0, 2))
    right = jnp.transpose(right_env, (1, 2, 0)).reshape(2, 384, 128)
    left = left_env.reshape(2048, 256)
    ops = jnp.transpose(mpo_ops, (1, 2, 0)).reshape(4, 48)
    vmem = pl.BlockSpec(memory_space=pltpu.VMEM)
    result = pl.pallas_call(
        kernel,
        out_shape=jax.ShapeDtypeStruct((2, 24, 256), BF16),
        in_specs=[vmem] * 6,
        out_specs=vmem,
        scratch_shapes=[
            pltpu.VMEM((16, 2, 128, 256), BF16),
            pltpu.VMEM((32, 2, 384, 128), BF16),
            pltpu.VMEM((16, 2, 2, 48, 1024), BF16),
            pltpu.VMEM((16, 48, 256), F32),
            pltpu.VMEM((256, 256), BF16),
            pltpu.VMEM((192, 256), F32),
            pltpu.VMEM((4, 192, 256), BF16),
            pltpu.VMEM((4, 192, 256), BF16),
            pltpu.VMEM((4, 192, 256), BF16),
            pltpu.VMEM((4, 192, 256), BF16),
            pltpu.VMEM((4, 48, 256), BF16),
            pltpu.VMEM((4, 48, 256), BF16),
            pltpu.SemaphoreType.DMA((N_COPIES,)),
            pltpu.SemaphoreType.DMA((N_COPIES,)),
            pltpu.SemaphoreType.DMA((4,)),
            pltpu.SemaphoreType.DMA((4,)),
        ],
        compiler_params=pltpu.CompilerParams(
            collective_id=0, has_side_effects=True, vmem_limit_bytes=48 * 1024 * 1024
        ),
        cost_estimate=pl.CostEstimate(flops=3_300_000_000, bytes_accessed=2_000_000, transcendentals=0),
        name="gradient_slab",
    )(site, right, left, mpo_out.reshape(1, 48), mpo_in.reshape(1, 48), ops)
    return jnp.transpose(result, (2, 0, 1))


def solution(mesh):
    return jax.shard_map(
        local,
        mesh=mesh,
        in_specs=(
            P("row", None, "col"),
            P(None, "row", "col"),
            P("row", None, "col"),
            P(),
            P(),
            P(),
        ),
        out_specs=P("col", None, "row"),
        check_vma=False,
    )
```

```python
import jax
import jax.numpy as jnp
from jax import lax
from jax.experimental import pallas as pl
from jax.experimental.pallas import tpu as pltpu
from jax.sharding import PartitionSpec as P

MESH = pl.DeviceIdType.MESH
BF16 = jnp.bfloat16
F32 = jnp.float32

RUNS = 3
N_COPIES = 144


def kernel(
    site_ref, right_hbm, left_hbm, out_idx_ref, in_idx_ref, ops_ref, result_ref,
    site_all, right_in, right_own, right_line, made_all, chan_all, left, mixed, expand,
    keep_k, keep_y, keep_x, done, to_k, from_k, to_y, from_y, to_x, from_x, to_z, from_z,
    send_sems, recv_sems, local_sems,
):
    r = lax.axis_index("row")
    c = lax.axis_index("col")
    x, zl, k = r // 8, (r // 2) % 4, r % 2
    y, zh = c // 4, c % 4

    def row_of(dx=0, dz=0, dk=0):
        return ((x + dx + 4) % 4) * 8 + ((zl + dz + 4) % 4) * 2 + (k + dk) % 2

    def col_of(dy=0, dz=0):
        return ((y + dy + 4) % 4) * 4 + (zh + dz + 4) % 4

    sibling = (row_of(dk=1), c)
    z_up, z_down = (r, col_of(dz=1)), (r, col_of(dz=-1))
    y_peers = [(r, col_of(dy=d)) for d in (1, 2, 3)]
    x_peers = [(row_of(dx=d), c) for d in (1, 2, 3)]
    line = [(row_of(dz=d), c) for d in (1, 2, 3)]
    y_up, y_down, x_up, x_down = y_peers[0], y_peers[2], x_peers[0], x_peers[2]

    barrier = pltpu.get_barrier_semaphore()
    partners = [sibling, z_up, z_down] + y_peers + x_peers + line
    for partner in partners:
        pl.semaphore_signal(barrier, inc=1, device_id=partner, device_id_type=MESH)

    fetch = pltpu.make_async_copy(right_hbm, right_in, local_sems.at[0])
    fetch.start()
    fetch_left = pltpu.make_async_copy(left_hbm.at[pl.ds(4 * y, 4)], left.at[y], local_sems.at[1])
    fetch_left.start()
    site_all[y, 0] = site_ref[...]
    fetch.wait()
    by_eight = right_in[...].astype(F32).reshape(16, 6, 8, 128)
    for p in range(RUNS):
        run = jnp.concatenate([by_eight[:, p], by_eight[:, 3 + p]], axis=1).astype(BF16)
        right_own[k, x, p] = run
    pl.semaphore_wait(barrier, len(partners))

    started = []

    def send(src, dst, device):
        n = len(started)
        copy = pltpu.make_async_remote_copy(
            src_ref=src, dst_ref=dst, send_sem=send_sems.at[n], recv_sem=recv_sems.at[n],
            device_id=device, device_id_type=MESH,
        )
        copy.start()
        started.append(copy)
        return n

    def arrive(n, dst, device):
        pltpu.make_async_remote_copy(
            src_ref=dst, dst_ref=dst, send_sem=send_sems.at[n], recv_sem=recv_sems.at[n],
            device_id=device, device_id_type=MESH,
        ).wait_recv()

    def to_peers(src, dst, peers, here):
        return [send(src((here + d) % 4), dst(here), peers[d - 1]) for d in (1, 2, 3)]

    def from_peers(copies, dst, peers, here):
        for d in (1, 2, 3):
            arrive(copies[d - 1], dst((here - d + 4) % 4), peers[4 - d - 1])

    def left_at(origin):
        return left.at[origin]

    class Ring:
        def __init__(self, own, low, high, far, up, down, half, places=None):
            self.own, self.low, self.high, self.far, self.up, self.down, self.half = own, low, high, far, up, down, half
            self.places = places or (own, own, half(low, 0), half(high, 1))

        def begin(self):
            self.n_up = send(self.own, self.places[0], self.up)
            self.n_down = send(self.own, self.places[1], self.down)

        def near(self):
            arrive(self.n_up, self.low, self.down)
            self.n_low = send(self.half(self.low, 0), self.places[2], self.up)
            arrive(self.n_down, self.high, self.up)
            self.n_high = send(self.half(self.high, 1), self.places[3], self.down)

        def end(self):
            arrive(self.n_low, self.half(self.far, 0), self.down)
            arrive(self.n_high, self.half(self.far, 1), self.up)

    def first_dim(ref, i):
        return ref.at[i]

    def two_of_four(ref, i):
        return ref.at[pl.ds(2 * i, 2)]

    def half_of_v(ref, i):
        return ref.at[:, pl.ds(8 * i, 8)]

    def x_ring(at):
        return Ring(at(x), at((x + 3) % 4), at((x + 1) % 4), at((x + 2) % 4), x_up, x_down, half_of_v)

    groups = {
        "own": lambda core, origin: right_own.at[core, origin],
        0: lambda core, origin: right_line.at[0, core, origin],
        1: lambda core, origin: right_line.at[1, core, origin],
        2: lambda core, origin: right_line.at[2, core, origin],
    }
    whole = {
        "own": lambda core: right_own.at[core],
        0: lambda core: right_line.at[0, core],
        1: lambda core: right_line.at[1, core],
        2: lambda core: right_line.at[2, core],
    }
    right_x, core_n, line_n = {}, {}, {}

    def x_begin(g):
        right_x[g] = x_ring(lambda origin: groups[g](k, origin))
        right_x[g].begin()

    def x_near(g):
        right_x[g].near()

    def x_end(g):
        right_x[g].end()
        core_n[g] = send(whole[g](k), whole[g](k), sibling)

    def core_end(g):
        arrive(core_n[g], whole[g](1 - k), sibling)

    def line_begin(p):
        line_n[p] = [
            send(right_own.at[k, x, p], right_line.at[p, k, x, d - 1], line[d - 1]) for d in (1, 2, 3)
        ]

    def line_end(p):
        for d in (1, 2, 3):
            arrive(line_n[p][d - 1], right_line.at[p, k, x, d - 1], line[4 - d - 1])

    site_y = {}

    def site_pass(part):
        at = {
            "own": lambda o: site_all.at[o, 0],
            "pair": lambda o: site_all.at[o, pl.ds(1, 2)],
            "far": lambda o: site_all.at[o, 3],
        }[part]
        site_y[part] = Ring(at(y), at((y + 3) % 4), at((y + 1) % 4), at((y + 2) % 4), y_up, y_down, first_dim)
        site_y[part].begin()

    x_begin("own")
    site_here = [site_all.at[y, q] for q in range(4)]
    site_z = Ring(
        site_here[0], site_here[2], site_here[1], site_here[3], z_up, z_down, first_dim,
        (site_here[2], site_here[1], site_here[3].at[0], site_here[3].at[1]),
    )
    site_z.begin()
    site_pass("own")
    left_n = to_peers(lambda to: left_hbm.at[pl.ds(4 * to, 4)], left_at, y_peers, y)

    channel_rows = lax.broadcasted_iota(jnp.int32, (16, 48), 0)
    pick_out = channel_rows == jnp.broadcast_to(out_idx_ref[...], (16, 48))
    pick_in = (channel_rows == jnp.broadcast_to(in_idx_ref[...], (16, 48))).astype(F32).astype(BF16)
    spread = (
        lax.broadcasted_iota(jnp.int32, (128, 16), 0) // 8 == lax.broadcasted_iota(jnp.int32, (128, 16), 1)
    ).astype(F32).astype(BF16)
    same = (lax.broadcasted_iota(jnp.int32, (128, 128), 0) % 8) == (lax.broadcasted_iota(jnp.int32, (128, 128), 1) % 8)
    for s in range(2):
        for t in range(2):
            op = ops_ref[pl.ds(2 * s + t, 1), :].astype(F32)
            picked = jnp.where(pick_out, jnp.broadcast_to(op, (16, 48)), 0.0).astype(BF16)
            dense = lax.dot_general(picked, pick_in, (((1,), (1,)), ((), ())), preferred_element_type=F32).astype(BF16)
            tall = jnp.dot(spread, dense, preferred_element_type=F32).astype(BF16)
            wide = lax.dot_general(tall, spread, (((1,), (1,)), ((), ())), preferred_element_type=F32)
            expand[pl.ds(128 * s, 128), pl.ds(128 * t, 128)] = jnp.where(same, wide, 0.0).astype(BF16)

    def make_channel(p):
        def right_block(core, g, d):
            block = right_own[core, g, p] if d == 0 else right_line[p, core, g, d - 1]
            return block.reshape(256, 128)

        mixed[...] = jnp.zeros_like(mixed)

        def add_blocks(g, carry):
            update = None
            for d in range(4):
                env = jnp.concatenate([right_block(0, g, d), right_block(1, g, d)], axis=1)
                step = (zl - d - zh + 8) % 4
                site = site_all[g, step + (step // 2) * (1 - 2 * (step % 2))].reshape(256, 256)
                term = lax.dot_general(env, site, (((1,), (1,)), ((), ())), preferred_element_type=F32)
                update = term if update is None else update + term
            mixed[...] += update
            return carry

        lax.fori_loop(0, 4, add_blocks, 0)
        by_eight = mixed[...].reshape(16, 2, 8, 256)
        stacked = []
        for i in range(2):
            run = by_eight[:, i].reshape(128, 256).astype(BF16)
            stacked.append(jnp.concatenate([run[:, :128], run[:, 128:]], axis=0))
        made = jnp.dot(expand[...], jnp.concatenate(stacked, axis=1), preferred_element_type=F32)
        for s in range(2):
            for group in range(4):
                pieces = []
                for w in range(4 * group, 4 * group + 4):
                    rows = made[s * 128 + w * 8:s * 128 + w * 8 + 8, :]
                    pieces.append(jnp.concatenate([rows[:, :128], rows[:, 128:]], axis=0))
                made_all[p, group, s] = jnp.concatenate(pieces, axis=1).astype(BF16)

    made_n = {}

    def spread_begin(p):
        run = pl.ds(2 * p, 2)
        chan_all[run, zh, y] = made_all[p, y]
        made_n[p] = to_peers(lambda to: made_all.at[p, to], lambda o: chan_all.at[run, zh, o], y_peers, y)

    def spread_end(p):
        from_peers(made_n[p], lambda o: chan_all.at[pl.ds(2 * p, 2), zh, o], y_peers, y)

    chan_z = {}

    def chan_begin(e, count):
        def at(origin):
            return chan_all.at[pl.ds(e, count), origin]

        chan_z[e] = Ring(
            at(zh), at((zh + 3) % 4), at((zh + 1) % 4), at((zh + 2) % 4), z_up, z_down,
            lambda ref, i: ref.at[:, pl.ds(2 * i, 2)],
        )
        chan_z[e].begin()

    k_n, y_n, x_n, z_n = {}, {}, {}, {}

    def share_k(e, count):
        part = pl.ds(e, count)
        rows = chan_all[part].reshape(count * 256, 512)
        for j in range(4):
            total = jnp.dot(rows, left[j].reshape(512, 256), preferred_element_type=F32)
            total = total.reshape(count * 16, 2, 8, 256)
            first, second = total[:, 0].reshape(count, 128, 256), total[:, 1].reshape(count, 128, 256)
            keep_k[j, part] = jnp.where(k == 0, first, second)
            to_k[part, j] = jnp.where(k == 0, second, first).astype(BF16)
        k_n[e] = send(to_k.at[part], from_k.at[part], sibling)

    def share_y(e, count):
        part = pl.ds(e, count)
        arrive(k_n[e], from_k.at[part], sibling)
        for d in (1, 3, 2):
            to = (y + d) % 4
            to_y[to, part] = (keep_k[to, part] + from_k[part, to].astype(F32)).astype(BF16)
        y_n[e] = to_peers(lambda to: to_y.at[to, part], lambda o: from_y.at[o, part], y_peers, y)
        keep_y[part] = keep_k[y, part] + from_k[part, y].astype(F32)

    def share_x(e, count):
        part = pl.ds(e, count)
        from_peers(y_n[e], lambda o: from_y.at[o, part], y_peers, y)
        total = keep_y[part]
        for d in (1, 3, 2):
            total = total + from_y[(y + d) % 4, part].astype(F32)
        total = total.reshape(count * 4, 4, 8, 256)
        for j in range(4):
            block = total[:, j].reshape(count, 32, 256)
            keep_x[j, part] = block
            to_x[j, part] = block.astype(BF16)
        x_n[e] = to_peers(lambda to: to_x.at[to, part], lambda o: from_x.at[o, part], x_peers, x)

    def share_z(e, count):
        part = pl.ds(e, count)
        from_peers(x_n[e], lambda o: from_x.at[o, part], x_peers, x)
        total = keep_x[x, part]
        for d in (1, 3, 2):
            total = total + from_x[(x + d) % 4, part].astype(F32)
        total = total.reshape(count, 4, 8, 256)
        for j in range(4):
            to_z[j, part] = total[:, j]
        z_n[e] = to_peers(lambda to: to_z.at[to, part], lambda o: from_z.at[o, part], line, zl)

    def share_end(e, count):
        part = pl.ds(e, count)
        from_peers(z_n[e], lambda o: from_z.at[o, part], line, zl)
        total = to_z[zl, part]
        for d in (1, 3, 2):
            total = total + from_z[(zl + d) % 4, part]
        done[part] = total

    def drain(upto):
        while drained[0] < upto:
            started[drained[0]].wait_send()
            drained[0] += 1

    drained = [0]
    x_near("own")
    site_y["own"].near()
    line_begin(0)
    x_end("own")
    site_y["own"].end()
    site_z.near()
    site_pass("pair")
    line_end(0)
    x_begin(0)
    site_y["pair"].near()
    site_z.end()
    site_pass("far")
    line_begin(1)
    x_near(0)
    site_y["pair"].end()
    x_end(0)
    site_y["far"].near()
    core_end("own")
    line_end(1)
    x_begin(1)
    line_begin(2)
    site_y["far"].end()
    core_end(0)

    make_channel(0)
    spread_begin(0)
    x_near(1)
    spread_end(0)
    chan_begin(0, 1)
    chan_begin(1, 1)
    x_end(1)
    line_end(2)
    x_begin(2)
    core_end(1)
    make_channel(1)
    spread_begin(1)
    spread_end(1)
    chan_begin(2, 1)
    chan_begin(3, 1)
    x_near(2)
    chan_z[0].near()
    x_end(2)
    chan_z[1].near()
    core_end(2)
    make_channel(2)
    spread_begin(2)
    chan_z[0].end()
    spread_end(2)
    chan_begin(4, 1)
    chan_begin(5, 1)
    chan_z[2].near()
    chan_z[1].end()
    fetch_left.wait()
    from_peers(left_n, left_at, y_peers, y)
    share_k(0, 2)
    chan_z[3].near()
    share_y(0, 2)
    drain(len(started) - 24)
    chan_z[2].end()
    share_x(0, 2)
    chan_z[4].near()
    chan_z[3].end()
    share_k(2, 2)
    drain(len(started) - 24)
    chan_z[5].near()
    share_y(2, 2)
    share_z(0, 2)
    chan_z[4].end()
    share_x(2, 2)
    chan_z[5].end()
    share_k(4, 2)
    share_z(2, 2)
    share_y(4, 2)
    share_end(0, 2)
    drain(len(started) - 24)
    share_x(4, 2)
    share_end(2, 2)
    drain(len(started) - 9)
    share_z(4, 2)
    drain(len(started) - 3)
    share_end(4, 2)
    for s in range(2):
        result_ref[s] = jnp.concatenate([done[2 * p + s] for p in range(RUNS)], axis=0).astype(BF16)
    drain(len(started))


def local(site_tensor, left_env, right_env, mpo_out, mpo_in, mpo_ops):
    site = jnp.transpose(site_tensor, (1, 0, 2))
    right = jnp.transpose(right_env, (1, 2, 0))
    ops = jnp.transpose(mpo_ops, (1, 2, 0)).reshape(4, 48)
    vmem = pl.BlockSpec(memory_space=pltpu.VMEM)
    hbm = pl.BlockSpec(memory_space=pl.ANY)
    result = pl.pallas_call(
        kernel,
        out_shape=jax.ShapeDtypeStruct((2, 24, 256), BF16),
        in_specs=[vmem, hbm, hbm, vmem, vmem, vmem],
        out_specs=vmem,
        scratch_shapes=[
            pltpu.VMEM((4, 4, 2, 128, 256), BF16),
            pltpu.VMEM((16, 48, 128), BF16),
            pltpu.VMEM((2, 4, RUNS, 16, 16, 128), BF16),
            pltpu.VMEM((RUNS, 2, 4, 3, 16, 16, 128), BF16),
            pltpu.VMEM((RUNS, 4, 2, 16, 512), BF16),
            pltpu.VMEM((2 * RUNS, 4, 4, 16, 512), BF16),
            pltpu.VMEM((4, 4, 128, 256), BF16),
            pltpu.VMEM((256, 256), F32),
            pltpu.VMEM((256, 256), BF16),
            pltpu.VMEM((4, 2 * RUNS, 128, 256), F32),
            pltpu.VMEM((2 * RUNS, 128, 256), F32),
            pltpu.VMEM((4, 2 * RUNS, 32, 256), F32),
            pltpu.VMEM((2 * RUNS, 8, 256), F32),
            pltpu.VMEM((2 * RUNS, 4, 128, 256), BF16),
            pltpu.VMEM((2 * RUNS, 4, 128, 256), BF16),
            pltpu.VMEM((4, 2 * RUNS, 128, 256), BF16),
            pltpu.VMEM((4, 2 * RUNS, 128, 256), BF16),
            pltpu.VMEM((4, 2 * RUNS, 32, 256), BF16),
            pltpu.VMEM((4, 2 * RUNS, 32, 256), BF16),
            pltpu.VMEM((4, 2 * RUNS, 8, 256), F32),
            pltpu.VMEM((4, 2 * RUNS, 8, 256), F32),
            pltpu.SemaphoreType.DMA((N_COPIES,)),
            pltpu.SemaphoreType.DMA((N_COPIES,)),
            pltpu.SemaphoreType.DMA((2,)),
        ],
        compiler_params=pltpu.CompilerParams(
            collective_id=0, has_side_effects=True, vmem_limit_bytes=62 * 1024 * 1024
        ),
        cost_estimate=pl.CostEstimate(flops=3_300_000_000, bytes_accessed=2_000_000, transcendentals=0),
        name="gradient_slab",
    )(site, right, left_env, mpo_out.reshape(1, 48), mpo_in.reshape(1, 48), ops)
    return jnp.transpose(result, (2, 0, 1))


def solution(mesh):
    return jax.shard_map(
        local,
        mesh=mesh,
        in_specs=(
            P("row", None, "col"),
            P(None, "row", "col"),
            P("row", None, "col"),
            P(),
            P(),
            P(),
        ),
        out_specs=P("col", None, "row"),
        check_vma=False,
    )
```

```python
import jax
import jax.numpy as jnp
from jax import lax
from jax.experimental import pallas as pl
from jax.experimental.pallas import tpu as pltpu
from jax.sharding import PartitionSpec as P

MESH = pl.DeviceIdType.MESH
BF16 = jnp.bfloat16
F32 = jnp.float32

RUNS = 3
N_COPIES = 144


def kernel(
    site_ref, right_hbm, left_hbm, out_idx_ref, in_idx_ref, ops_ref, result_ref,
    site_all, right_in, right_own, right_line, made_all, chan_all, left, mixed, expand,
    keep_k, keep_y, keep_x, done, keep_first, to_k, from_k, to_first, from_first, to_y, from_y, to_x, from_x, to_z, from_z,
    send_sems, recv_sems, local_sems,
):
    r = lax.axis_index("row")
    c = lax.axis_index("col")
    x, zl, k = r // 8, (r // 2) % 4, r % 2
    y, zh = c // 4, c % 4

    def row_of(dx=0, dz=0, dk=0):
        return ((x + dx + 4) % 4) * 8 + ((zl + dz + 4) % 4) * 2 + (k + dk) % 2

    def col_of(dy=0, dz=0):
        return ((y + dy + 4) % 4) * 4 + (zh + dz + 4) % 4

    sibling = (row_of(dk=1), c)
    z_up, z_down = (r, col_of(dz=1)), (r, col_of(dz=-1))
    y_peers = [(r, col_of(dy=d)) for d in (1, 2, 3)]
    x_peers = [(row_of(dx=d), c) for d in (1, 2, 3)]
    line = [(row_of(dz=d), c) for d in (1, 2, 3)]
    y_up, y_down, x_up, x_down = y_peers[0], y_peers[2], x_peers[0], x_peers[2]

    barrier = pltpu.get_barrier_semaphore()
    partners = [sibling, z_up, z_down] + y_peers + x_peers + line
    for partner in partners:
        pl.semaphore_signal(barrier, inc=1, device_id=partner, device_id_type=MESH)

    fetch = pltpu.make_async_copy(right_hbm, right_in, local_sems.at[0])
    fetch.start()
    fetch_left = pltpu.make_async_copy(left_hbm.at[pl.ds(4 * y, 4)], left.at[y], local_sems.at[1])
    fetch_left.start()
    for t in range(2):
        site_all[y, 0, t] = site_ref[:, t, :]
    fetch.wait()
    by_eight = right_in[...].astype(F32).reshape(16, 6, 8, 128)
    for p in range(RUNS):
        run = jnp.concatenate([by_eight[:, p], by_eight[:, 3 + p]], axis=1).astype(BF16)
        right_own[k, x, p] = run
    pl.semaphore_wait(barrier, len(partners))

    started = []

    def send(src, dst, device):
        n = len(started)
        copy = pltpu.make_async_remote_copy(
            src_ref=src, dst_ref=dst, send_sem=send_sems.at[n], recv_sem=recv_sems.at[n],
            device_id=device, device_id_type=MESH,
        )
        copy.start()
        started.append(copy)
        return n

    def arrive(n, dst, device):
        pltpu.make_async_remote_copy(
            src_ref=dst, dst_ref=dst, send_sem=send_sems.at[n], recv_sem=recv_sems.at[n],
            device_id=device, device_id_type=MESH,
        ).wait_recv()

    def to_peers(src, dst, peers, here):
        return [send(src((here + d) % 4), dst(here), peers[d - 1]) for d in (1, 2, 3)]

    def from_peers(copies, dst, peers, here):
        for d in (1, 2, 3):
            arrive(copies[d - 1], dst((here - d + 4) % 4), peers[4 - d - 1])

    def left_at(origin):
        return left.at[origin]

    class Ring:
        def __init__(self, own, low, high, far, up, down, half, places=None):
            self.own, self.low, self.high, self.far, self.up, self.down, self.half = own, low, high, far, up, down, half
            self.places = places or (own, own, half(low, 0), half(high, 1))

        def begin(self):
            self.n_up = send(self.own, self.places[0], self.up)
            self.n_down = send(self.own, self.places[1], self.down)

        def near(self):
            arrive(self.n_up, self.low, self.down)
            self.n_low = send(self.half(self.low, 0), self.places[2], self.up)
            arrive(self.n_down, self.high, self.up)
            self.n_high = send(self.half(self.high, 1), self.places[3], self.down)

        def end(self):
            arrive(self.n_low, self.half(self.far, 0), self.down)
            arrive(self.n_high, self.half(self.far, 1), self.up)

    def first_dim(ref, i):
        return ref.at[i]

    def two_of_four(ref, i):
        return ref.at[pl.ds(2 * i, 2)]

    def half_of_v(ref, i):
        return ref.at[:, pl.ds(8 * i, 8)]

    def x_ring(at):
        return Ring(at(x), at((x + 3) % 4), at((x + 1) % 4), at((x + 2) % 4), x_up, x_down, half_of_v)

    groups = {
        "own": lambda core, origin: right_own.at[core, origin],
        0: lambda core, origin: right_line.at[0, core, origin],
        1: lambda core, origin: right_line.at[1, core, origin],
        2: lambda core, origin: right_line.at[2, core, origin],
    }
    whole = {
        "own": lambda core: right_own.at[core],
        0: lambda core: right_line.at[0, core],
        1: lambda core: right_line.at[1, core],
        2: lambda core: right_line.at[2, core],
    }
    right_x, core_n, line_n = {}, {}, {}

    def x_begin(g):
        right_x[g] = x_ring(lambda origin: groups[g](k, origin))
        right_x[g].begin()

    def x_near(g):
        right_x[g].near()

    def x_end(g):
        right_x[g].end()
        core_n[g] = send(whole[g](k), whole[g](k), sibling)

    def core_end(g):
        arrive(core_n[g], whole[g](1 - k), sibling)

    def line_begin(p):
        line_n[p] = [
            send(right_own.at[k, x, p], right_line.at[p, k, x, d - 1], line[d - 1]) for d in (1, 2, 3)
        ]

    def line_end(p):
        for d in (1, 2, 3):
            arrive(line_n[p][d - 1], right_line.at[p, k, x, d - 1], line[4 - d - 1])

    site_y = {}

    def site_pass(part):
        at = {
            "own": lambda o: site_all.at[o, 0],
            "pair": lambda o: site_all.at[o, pl.ds(1, 2)],
            "far": lambda o: site_all.at[o, 3],
        }[part]
        site_y[part] = Ring(at(y), at((y + 3) % 4), at((y + 1) % 4), at((y + 2) % 4), y_up, y_down, first_dim)
        site_y[part].begin()

    x_begin("own")
    site_here = [site_all.at[y, q] for q in range(4)]
    site_z = Ring(
        site_here[0], site_here[2], site_here[1], site_here[3], z_up, z_down, first_dim,
        (site_here[2], site_here[1], site_here[3].at[0], site_here[3].at[1]),
    )
    site_z.begin()
    site_pass("own")
    left_n = to_peers(lambda to: left_hbm.at[pl.ds(4 * to, 4)], left_at, y_peers, y)

    channel_rows = lax.broadcasted_iota(jnp.int32, (16, 48), 0)
    pick_out = channel_rows == jnp.broadcast_to(out_idx_ref[...], (16, 48))
    pick_in = (channel_rows == jnp.broadcast_to(in_idx_ref[...], (16, 48))).astype(F32).astype(BF16)
    spread = (
        lax.broadcasted_iota(jnp.int32, (128, 16), 0) // 8 == lax.broadcasted_iota(jnp.int32, (128, 16), 1)
    ).astype(F32).astype(BF16)
    same = (lax.broadcasted_iota(jnp.int32, (128, 128), 0) % 8) == (lax.broadcasted_iota(jnp.int32, (128, 128), 1) % 8)
    for s in range(2):
        for t in range(2):
            op = ops_ref[pl.ds(2 * s + t, 1), :].astype(F32)
            picked = jnp.where(pick_out, jnp.broadcast_to(op, (16, 48)), 0.0).astype(BF16)
            dense = lax.dot_general(picked, pick_in, (((1,), (1,)), ((), ())), preferred_element_type=F32).astype(BF16)
            tall = jnp.dot(spread, dense, preferred_element_type=F32).astype(BF16)
            wide = lax.dot_general(tall, spread, (((1,), (1,)), ((), ())), preferred_element_type=F32)
            expand[pl.ds(128 * s, 128), pl.ds(128 * t, 128)] = jnp.where(same, wide, 0.0).astype(BF16)

    def make_channel(p):
        def right_block(core, g, d):
            block = right_own[core, g, p] if d == 0 else right_line[p, core, g, d - 1]
            return block.reshape(256, 128)

        mixed[...] = jnp.zeros_like(mixed)

        def add_blocks(g, carry):
            update = None
            for d in range(4):
                env = jnp.concatenate([right_block(0, g, d), right_block(1, g, d)], axis=1)
                step = (zl - d - zh + 8) % 4
                site = site_all[g, step + (step // 2) * (1 - 2 * (step % 2))].reshape(256, 256)
                term = lax.dot_general(env, site, (((1,), (1,)), ((), ())), preferred_element_type=F32)
                update = term if update is None else update + term
            mixed[...] += update
            return carry

        lax.fori_loop(0, 4, add_blocks, 0)
        by_eight = mixed[...].reshape(16, 2, 8, 256)
        stacked = []
        for i in range(2):
            run = by_eight[:, i].reshape(128, 256).astype(BF16)
            stacked.append(jnp.concatenate([run[:, :128], run[:, 128:]], axis=0))
        made = jnp.dot(expand[...], jnp.concatenate(stacked, axis=1), preferred_element_type=F32)
        for s in range(2):
            for group in range(4):
                pieces = []
                for w in range(4 * group, 4 * group + 4):
                    rows = made[s * 128 + w * 8:s * 128 + w * 8 + 8, :]
                    pieces.append(jnp.concatenate([rows[:, :128], rows[:, 128:]], axis=0))
                made_all[p, group, s] = jnp.concatenate(pieces, axis=1).astype(BF16)

    made_n = {}

    def spread_begin(p):
        run = pl.ds(2 * p, 2)
        chan_all[run, zh, y] = made_all[p, y]
        made_n[p] = to_peers(lambda to: made_all.at[p, to], lambda o: chan_all.at[run, zh, o], y_peers, y)

    def spread_end(p):
        from_peers(made_n[p], lambda o: chan_all.at[pl.ds(2 * p, 2), zh, o], y_peers, y)

    chan_z = {}

    def chan_begin(e, count):
        def at(origin):
            return chan_all.at[pl.ds(e, count), origin]

        chan_z[e] = Ring(
            at(zh), at((zh + 3) % 4), at((zh + 1) % 4), at((zh + 2) % 4), z_up, z_down,
            lambda ref, i: ref.at[:, pl.ds(2 * i, 2)],
        )
        chan_z[e].begin()

    k_n, y_n, x_n, z_n = {}, {}, {}, {}

    def share_k(e, count):
        part = pl.ds(e, count)
        rows = chan_all[part].reshape(count * 256, 512)
        for j in range(4):
            total = jnp.dot(rows, left[j].reshape(512, 256), preferred_element_type=F32)
            total = total.reshape(count * 16, 2, 8, 256)
            first, second = total[:, 0].reshape(count, 128, 256), total[:, 1].reshape(count, 128, 256)
            keep_k[j, part] = jnp.where(k == 0, first, second)
            to_k[part, j] = jnp.where(k == 0, second, first).astype(BF16)
        k_n[e] = send(to_k.at[part], from_k.at[part], sibling)

    def share_y(e, count):
        part = pl.ds(e, count)
        arrive(k_n[e], from_k.at[part], sibling)
        for d in (1, 3, 2):
            to = (y + d) % 4
            to_y[to, part] = (keep_k[to, part] + from_k[part, to].astype(F32)).astype(BF16)
        y_n[e] = to_peers(lambda to: to_y.at[to, part], lambda o: from_y.at[o, part], y_peers, y)
        keep_y[part] = keep_k[y, part] + from_k[part, y].astype(F32)

    def share_x(e, count):
        part = pl.ds(e, count)
        from_peers(y_n[e], lambda o: from_y.at[o, part], y_peers, y)
        total = keep_y[part]
        for d in (1, 3, 2):
            total = total + from_y[(y + d) % 4, part].astype(F32)
        total = total.reshape(count * 4, 4, 8, 256)
        for j in range(4):
            block = total[:, j].reshape(count, 32, 256)
            keep_x[j, part] = block
            to_x[j, part] = block.astype(BF16)
        x_n[e] = to_peers(lambda to: to_x.at[to, part], lambda o: from_x.at[o, part], x_peers, x)

    def share_x_first(e, count):
        part = pl.ds(e, count)
        arrive(k_n[e], from_k.at[part], sibling)
        for j in range(4):
            total = (keep_k[j, part] + from_k[part, j].astype(F32)).reshape(count * 4, 4, 8, 256)
            for to in range(4):
                block = total[:, to].reshape(count, 32, 256)
                keep_first[to, part, j] = block
                to_first[to, part, j] = block.astype(BF16)
        x_n[e] = to_peers(lambda to: to_first.at[to, part], lambda o: from_first.at[o, part], x_peers, x)

    def share_y_second(e, count):
        part = pl.ds(e, count)
        from_peers(x_n[e], lambda o: from_first.at[o, part], x_peers, x)
        for j in range(4):
            total = keep_first[x, part, j]
            for d in (1, 3, 2):
                total = total + from_first[(x + d) % 4, part, j].astype(F32)
            keep_x[j, part] = total
            to_x[j, part] = total.astype(BF16)
        y_n[e] = to_peers(lambda to: to_x.at[to, part], lambda o: from_x.at[o, part], y_peers, y)

    def share_z(e, count, x_first=False):
        part = pl.ds(e, count)
        here = y if x_first else x
        from_peers((y_n if x_first else x_n)[e], lambda o: from_x.at[o, part], y_peers if x_first else x_peers, here)
        total = keep_x[here, part]
        for d in (1, 3, 2):
            total = total + from_x[(here + d) % 4, part].astype(F32)
        total = total.reshape(count, 4, 8, 256)
        for j in range(4):
            to_z[j, part] = total[:, j]
        z_n[e] = to_peers(lambda to: to_z.at[to, part], lambda o: from_z.at[o, part], line, zl)

    def share_end(e, count):
        part = pl.ds(e, count)
        from_peers(z_n[e], lambda o: from_z.at[o, part], line, zl)
        total = to_z[zl, part]
        for d in (1, 3, 2):
            total = total + from_z[(zl + d) % 4, part]
        done[part] = total

    def drain(upto):
        while drained[0] < upto:
            started[drained[0]].wait_send()
            drained[0] += 1

    drained = [0]
    x_near("own")
    site_y["own"].near()
    line_begin(0)
    x_end("own")
    site_z.near()
    site_pass("pair")
    site_y["own"].end()
    line_end(0)
    x_begin(0)
    site_y["pair"].near()
    site_z.end()
    site_pass("far")
    line_begin(1)
    x_near(0)
    site_y["pair"].end()
    x_end(0)
    site_y["far"].near()
    core_end("own")
    line_end(1)
    x_begin(1)
    line_begin(2)
    site_y["far"].end()
    core_end(0)

    make_channel(0)
    spread_begin(0)
    x_near(1)
    spread_end(0)
    chan_begin(0, 1)
    chan_begin(1, 1)
    x_end(1)
    line_end(2)
    x_begin(2)
    core_end(1)
    make_channel(1)
    spread_begin(1)
    spread_end(1)
    chan_begin(2, 1)
    chan_begin(3, 1)
    x_near(2)
    chan_z[0].near()
    x_end(2)
    chan_z[1].near()
    core_end(2)
    make_channel(2)
    spread_begin(2)
    spread_end(2)
    chan_begin(4, 1)
    chan_begin(5, 1)
    drain(len(started) - 24)
    chan_z[2].near()
    chan_z[3].near()
    chan_z[0].end()
    chan_z[1].end()
    fetch_left.wait()
    from_peers(left_n, left_at, y_peers, y)
    share_k(0, 2)
    drain(len(started) - 16)
    share_y(0, 2)
    chan_z[4].near()
    chan_z[5].near()
    chan_z[2].end()
    chan_z[3].end()
    share_k(2, 2)
    share_x(0, 2)
    share_x_first(2, 2)
    chan_z[4].end()
    share_k(4, 1)
    share_y(4, 1)
    chan_z[5].end()
    share_k(5, 1)
    share_z(0, 2)
    share_x_first(5, 1)
    share_y_second(2, 2)
    share_x(4, 1)
    share_y_second(5, 1)
    share_z(2, 2, True)
    share_z(4, 1)
    share_z(5, 1, True)
    share_end(0, 2)
    drain(len(started) - 16)
    share_end(2, 2)
    share_end(4, 1)
    drain(len(started) - 3)
    share_end(5, 1)
    for s in range(2):
        result_ref[s] = jnp.concatenate([done[2 * p + s] for p in range(RUNS)], axis=0).astype(BF16)
    drain(len(started))


def local(site_tensor, left_env, right_env, mpo_out, mpo_in, mpo_ops):
    right = jnp.transpose(right_env, (1, 2, 0))
    ops = jnp.transpose(mpo_ops, (1, 2, 0)).reshape(4, 48)
    vmem = pl.BlockSpec(memory_space=pltpu.VMEM)
    hbm = pl.BlockSpec(memory_space=pl.ANY)
    result = pl.pallas_call(
        kernel,
        out_shape=jax.ShapeDtypeStruct((2, 24, 256), BF16),
        in_specs=[vmem, hbm, hbm, vmem, vmem, vmem],
        out_specs=vmem,
        scratch_shapes=[
            pltpu.VMEM((4, 4, 2, 128, 256), BF16),
            pltpu.VMEM((16, 48, 128), BF16),
            pltpu.VMEM((2, 4, RUNS, 16, 16, 128), BF16),
            pltpu.VMEM((RUNS, 2, 4, 3, 16, 16, 128), BF16),
            pltpu.VMEM((RUNS, 4, 2, 16, 512), BF16),
            pltpu.VMEM((2 * RUNS, 4, 4, 16, 512), BF16),
            pltpu.VMEM((4, 4, 128, 256), BF16),
            pltpu.VMEM((256, 256), F32),
            pltpu.VMEM((256, 256), BF16),
            pltpu.VMEM((4, 2 * RUNS, 128, 256), F32),
            pltpu.VMEM((2 * RUNS, 128, 256), F32),
            pltpu.VMEM((4, 2 * RUNS, 32, 256), F32),
            pltpu.VMEM((2 * RUNS, 8, 256), F32),
            pltpu.VMEM((4, 2 * RUNS, 4, 32, 256), F32),
            pltpu.VMEM((2 * RUNS, 4, 128, 256), BF16),
            pltpu.VMEM((2 * RUNS, 4, 128, 256), BF16),
            pltpu.VMEM((4, 2 * RUNS, 4, 32, 256), BF16),
            pltpu.VMEM((4, 2 * RUNS, 4, 32, 256), BF16),
            pltpu.VMEM((4, 2 * RUNS, 128, 256), BF16),
            pltpu.VMEM((4, 2 * RUNS, 128, 256), BF16),
            pltpu.VMEM((4, 2 * RUNS, 32, 256), BF16),
            pltpu.VMEM((4, 2 * RUNS, 32, 256), BF16),
            pltpu.VMEM((4, 2 * RUNS, 8, 256), F32),
            pltpu.VMEM((4, 2 * RUNS, 8, 256), F32),
            pltpu.SemaphoreType.DMA((N_COPIES,)),
            pltpu.SemaphoreType.DMA((N_COPIES,)),
            pltpu.SemaphoreType.DMA((2,)),
        ],
        compiler_params=pltpu.CompilerParams(
            collective_id=0, has_side_effects=True, vmem_limit_bytes=62 * 1024 * 1024
        ),
        cost_estimate=pl.CostEstimate(flops=3_300_000_000, bytes_accessed=2_000_000, transcendentals=0),
        name="gradient_slab",
    )(site_tensor, right, left_env, mpo_out.reshape(1, 48), mpo_in.reshape(1, 48), ops)
    return jnp.transpose(result, (2, 0, 1))


def solution(mesh):
    return jax.shard_map(
        local,
        mesh=mesh,
        in_specs=(
            P("row", None, "col"),
            P(None, "row", "col"),
            P("row", None, "col"),
            P(),
            P(),
            P(),
        ),
        out_specs=P("col", None, "row"),
        check_vma=False,
    )
```

```python
import jax
import jax.numpy as jnp
from jax import lax
from jax.experimental import pallas as pl
from jax.experimental.pallas import tpu as pltpu
from jax.sharding import PartitionSpec as P

MESH = pl.DeviceIdType.MESH
BF16 = jnp.bfloat16
F32 = jnp.float32

RUNS = 3
N_COPIES = 144


def kernel(
    site_ref, right_hbm, left_hbm, out_idx_ref, in_idx_ref, ops_ref, result_ref,
    site_all, right_in, right_own, right_line, made_first, made_all, chan_all, left, mixed, expand,
    keep_k, keep_y, keep_x, done, keep_first, to_k, from_k, to_first, from_first, to_y, from_y, to_x, from_x, to_z, from_z,
    send_sems, recv_sems, local_sems,
):
    r = lax.axis_index("row")
    c = lax.axis_index("col")
    x, zl, k = r // 8, (r // 2) % 4, r % 2
    y, zh = c // 4, c % 4

    def row_of(dx=0, dz=0, dk=0):
        return ((x + dx + 4) % 4) * 8 + ((zl + dz + 4) % 4) * 2 + (k + dk) % 2

    def col_of(dy=0, dz=0):
        return ((y + dy + 4) % 4) * 4 + (zh + dz + 4) % 4

    sibling = (row_of(dk=1), c)
    z_up, z_down = (r, col_of(dz=1)), (r, col_of(dz=-1))
    y_peers = [(r, col_of(dy=d)) for d in (1, 2, 3)]
    x_peers = [(row_of(dx=d), c) for d in (1, 2, 3)]
    line = [(row_of(dz=d), c) for d in (1, 2, 3)]
    y_up, y_down, x_up, x_down = y_peers[0], y_peers[2], x_peers[0], x_peers[2]

    barrier = pltpu.get_barrier_semaphore()
    partners = [sibling, z_up, z_down] + y_peers + x_peers + line
    for partner in partners:
        pl.semaphore_signal(barrier, inc=1, device_id=partner, device_id_type=MESH)

    fetch = pltpu.make_async_copy(right_hbm, right_in, local_sems.at[0])
    fetch.start()
    fetch_left = pltpu.make_async_copy(left_hbm.at[pl.ds(4 * y, 4)], left.at[y], local_sems.at[1])
    fetch_left.start()
    for t in range(2):
        site_all[y, 0, t] = site_ref[:, t, :]
    fetch.wait()
    by_eight = right_in[...].astype(F32).reshape(16, 6, 8, 128)
    for p in range(RUNS):
        run = jnp.concatenate([by_eight[:, p], by_eight[:, 3 + p]], axis=1).astype(BF16)
        right_own[k, x, p] = run
    pl.semaphore_wait(barrier, len(partners))

    started = []

    def send(src, dst, device):
        n = len(started)
        copy = pltpu.make_async_remote_copy(
            src_ref=src, dst_ref=dst, send_sem=send_sems.at[n], recv_sem=recv_sems.at[n],
            device_id=device, device_id_type=MESH,
        )
        copy.start()
        started.append(copy)
        return n

    def arrive(n, dst, device):
        pltpu.make_async_remote_copy(
            src_ref=dst, dst_ref=dst, send_sem=send_sems.at[n], recv_sem=recv_sems.at[n],
            device_id=device, device_id_type=MESH,
        ).wait_recv()

    def to_peers(src, dst, peers, here):
        return [send(src((here + d) % 4), dst(here), peers[d - 1]) for d in (1, 2, 3)]

    def from_peers(copies, dst, peers, here):
        for d in (1, 2, 3):
            arrive(copies[d - 1], dst((here - d + 4) % 4), peers[4 - d - 1])

    def left_at(origin):
        return left.at[origin]

    class Ring:
        def __init__(self, own, low, high, far, up, down, half, places=None):
            self.own, self.low, self.high, self.far, self.up, self.down, self.half = own, low, high, far, up, down, half
            self.places = places or (own, own, half(low, 0), half(high, 1))

        def begin(self):
            self.n_up = send(self.own, self.places[0], self.up)
            self.n_down = send(self.own, self.places[1], self.down)

        def near(self):
            arrive(self.n_up, self.low, self.down)
            self.n_low = send(self.half(self.low, 0), self.places[2], self.up)
            arrive(self.n_down, self.high, self.up)
            self.n_high = send(self.half(self.high, 1), self.places[3], self.down)

        def end(self):
            arrive(self.n_low, self.half(self.far, 0), self.down)
            arrive(self.n_high, self.half(self.far, 1), self.up)

    def first_dim(ref, i):
        return ref.at[i]

    def two_of_four(ref, i):
        return ref.at[pl.ds(2 * i, 2)]

    def half_of_v(ref, i):
        return ref.at[:, pl.ds(8 * i, 8)]

    def x_ring(at):
        return Ring(at(x), at((x + 3) % 4), at((x + 1) % 4), at((x + 2) % 4), x_up, x_down, half_of_v)

    groups = {
        "own": lambda core, origin: right_own.at[core, origin],
        0: lambda core, origin: right_line.at[0, core, origin],
        1: lambda core, origin: right_line.at[1, core, origin],
        2: lambda core, origin: right_line.at[2, core, origin],
    }
    whole = {
        "own": lambda core: right_own.at[core],
        0: lambda core: right_line.at[0, core],
        1: lambda core: right_line.at[1, core],
        2: lambda core: right_line.at[2, core],
    }
    right_x, core_n, line_n = {}, {}, {}

    def x_begin(g):
        right_x[g] = x_ring(lambda origin: groups[g](k, origin))
        right_x[g].begin()

    def x_near(g):
        right_x[g].near()

    def x_end(g):
        right_x[g].end()
        core_n[g] = send(whole[g](k), whole[g](k), sibling)

    def core_end(g):
        arrive(core_n[g], whole[g](1 - k), sibling)

    def line_begin(p):
        line_n[p] = [
            send(right_own.at[k, x, p], right_line.at[p, k, x, d - 1], line[d - 1]) for d in (1, 2, 3)
        ]

    def line_end(p):
        for d in (1, 2, 3):
            arrive(line_n[p][d - 1], right_line.at[p, k, x, d - 1], line[4 - d - 1])

    site_y = {}

    def site_pass(part):
        at = {
            "own": lambda o: site_all.at[o, 0],
            "pair": lambda o: site_all.at[o, pl.ds(1, 2)],
            "far": lambda o: site_all.at[o, 3],
        }[part]
        site_y[part] = Ring(at(y), at((y + 3) % 4), at((y + 1) % 4), at((y + 2) % 4), y_up, y_down, first_dim)
        site_y[part].begin()

    x_begin("own")
    site_here = [site_all.at[y, q] for q in range(4)]
    site_z = Ring(
        site_here[0], site_here[2], site_here[1], site_here[3], z_up, z_down, first_dim,
        (site_here[2], site_here[1], site_here[3].at[0], site_here[3].at[1]),
    )
    site_z.begin()
    site_pass("own")
    left_n = to_peers(lambda to: left_hbm.at[pl.ds(4 * to, 4)], left_at, y_peers, y)

    channel_rows = lax.broadcasted_iota(jnp.int32, (16, 48), 0)
    pick_out = channel_rows == jnp.broadcast_to(out_idx_ref[...], (16, 48))
    pick_in = (channel_rows == jnp.broadcast_to(in_idx_ref[...], (16, 48))).astype(F32).astype(BF16)
    spread = (
        lax.broadcasted_iota(jnp.int32, (128, 16), 0) // 8 == lax.broadcasted_iota(jnp.int32, (128, 16), 1)
    ).astype(F32).astype(BF16)
    same = (lax.broadcasted_iota(jnp.int32, (128, 128), 0) % 8) == (lax.broadcasted_iota(jnp.int32, (128, 128), 1) % 8)
    for s in range(2):
        for t in range(2):
            op = ops_ref[pl.ds(2 * s + t, 1), :].astype(F32)
            picked = jnp.where(pick_out, jnp.broadcast_to(op, (16, 48)), 0.0).astype(BF16)
            dense = lax.dot_general(picked, pick_in, (((1,), (1,)), ((), ())), preferred_element_type=F32).astype(BF16)
            tall = jnp.dot(spread, dense, preferred_element_type=F32).astype(BF16)
            wide = lax.dot_general(tall, spread, (((1,), (1,)), ((), ())), preferred_element_type=F32)
            expand[pl.ds(128 * s, 128), pl.ds(128 * t, 128)] = jnp.where(same, wide, 0.0).astype(BF16)

    def make_channel(p):
        def right_block(core, g, d):
            block = right_own[core, g, p] if d == 0 else right_line[p, core, g, d - 1]
            return block.reshape(256, 128)

        mixed[...] = jnp.zeros_like(mixed)

        def add_blocks(g, carry):
            update = None
            for d in range(4):
                env = jnp.concatenate([right_block(0, g, d), right_block(1, g, d)], axis=1)
                step = (zl - d - zh + 8) % 4
                site = site_all[g, step + (step // 2) * (1 - 2 * (step % 2))].reshape(256, 256)
                term = lax.dot_general(env, site, (((1,), (1,)), ((), ())), preferred_element_type=F32)
                update = term if update is None else update + term
            mixed[...] += update
            return carry

        lax.fori_loop(0, 4, add_blocks, 0)
        by_eight = mixed[...].reshape(16, 2, 8, 256)
        stacked = []
        for i in range(2):
            run = by_eight[:, i].reshape(128, 256).astype(BF16)
            stacked.append(jnp.concatenate([run[:, :128], run[:, 128:]], axis=0))
        made = jnp.dot(expand[...], jnp.concatenate(stacked, axis=1), preferred_element_type=F32)
        for s in range(2):
            for group in range(4):
                pieces = []
                for w in range(4 * group, 4 * group + 4):
                    rows = made[s * 128 + w * 8:s * 128 + w * 8 + 8, :]
                    pieces.append(jnp.concatenate([rows[:, :128], rows[:, 128:]], axis=0))
                rows = jnp.concatenate(pieces, axis=1).astype(BF16)
                if p == 0:
                    made_first[zh, group, s] = rows
                else:
                    made_all[p, group, s] = rows

    made_n = {}

    def spread_begin(p):
        run = pl.ds(2 * p, 2)
        chan_all[run, zh, y] = made_all[p, y]
        made_n[p] = to_peers(lambda to: made_all.at[p, to], lambda o: chan_all.at[run, zh, o], y_peers, y)

    def spread_end(p):
        from_peers(made_n[p], lambda o: chan_all.at[pl.ds(2 * p, 2), zh, o], y_peers, y)

    first = Ring(
        made_first.at[zh], made_first.at[(zh + 3) % 4], made_first.at[(zh + 1) % 4], made_first.at[(zh + 2) % 4],
        z_up, z_down, two_of_four,
    )
    first_n = {}

    def first_spread(dz):
        origin = (zh + dz) % 4
        chan_all[pl.ds(0, 2), origin, y] = made_first[origin, y]
        first_n[dz] = to_peers(
            lambda to: made_first.at[origin, to], lambda o: chan_all.at[pl.ds(0, 2), origin, o], y_peers, y
        )

    def first_spread_end(dz):
        origin = (zh + dz) % 4
        from_peers(first_n[dz], lambda o: chan_all.at[pl.ds(0, 2), origin, o], y_peers, y)

    chan_z = {}

    def chan_begin(e, count):
        def at(origin):
            return chan_all.at[pl.ds(e, count), origin]

        chan_z[e] = Ring(
            at(zh), at((zh + 3) % 4), at((zh + 1) % 4), at((zh + 2) % 4), z_up, z_down,
            lambda ref, i: ref.at[:, pl.ds(2 * i, 2)],
        )
        chan_z[e].begin()

    k_n, y_n, x_n, z_n = {}, {}, {}, {}

    def share_k(e, count):
        part = pl.ds(e, count)
        rows = chan_all[part].reshape(count * 256, 512)
        for j in range(4):
            total = jnp.dot(rows, left[j].reshape(512, 256), preferred_element_type=F32)
            total = total.reshape(count * 16, 2, 8, 256)
            first, second = total[:, 0].reshape(count, 128, 256), total[:, 1].reshape(count, 128, 256)
            keep_k[j, part] = jnp.where(k == 0, first, second)
            to_k[part, j] = jnp.where(k == 0, second, first).astype(BF16)
        k_n[e] = send(to_k.at[part], from_k.at[part], sibling)

    def share_y(e, count):
        part = pl.ds(e, count)
        arrive(k_n[e], from_k.at[part], sibling)
        for d in (1, 3, 2):
            to = (y + d) % 4
            to_y[to, part] = (keep_k[to, part] + from_k[part, to].astype(F32)).astype(BF16)
        y_n[e] = to_peers(lambda to: to_y.at[to, part], lambda o: from_y.at[o, part], y_peers, y)
        keep_y[part] = keep_k[y, part] + from_k[part, y].astype(F32)

    def share_x(e, count):
        part = pl.ds(e, count)
        from_peers(y_n[e], lambda o: from_y.at[o, part], y_peers, y)
        total = keep_y[part]
        for d in (1, 3, 2):
            total = total + from_y[(y + d) % 4, part].astype(F32)
        total = total.reshape(count * 4, 4, 8, 256)
        for j in range(4):
            block = total[:, j].reshape(count, 32, 256)
            keep_x[j, part] = block
            to_x[j, part] = block.astype(BF16)
        x_n[e] = to_peers(lambda to: to_x.at[to, part], lambda o: from_x.at[o, part], x_peers, x)

    def share_x_first(e, count):
        part = pl.ds(e, count)
        arrive(k_n[e], from_k.at[part], sibling)
        for j in range(4):
            total = (keep_k[j, part] + from_k[part, j].astype(F32)).reshape(count * 4, 4, 8, 256)
            for to in range(4):
                block = total[:, to].reshape(count, 32, 256)
                keep_first[to, part, j] = block
                to_first[to, part, j] = block.astype(BF16)
        x_n[e] = to_peers(lambda to: to_first.at[to, part], lambda o: from_first.at[o, part], x_peers, x)

    def share_y_second(e, count):
        part = pl.ds(e, count)
        from_peers(x_n[e], lambda o: from_first.at[o, part], x_peers, x)
        for j in range(4):
            total = keep_first[x, part, j]
            for d in (1, 3, 2):
                total = total + from_first[(x + d) % 4, part, j].astype(F32)
            keep_x[j, part] = total
            to_x[j, part] = total.astype(BF16)
        y_n[e] = to_peers(lambda to: to_x.at[to, part], lambda o: from_x.at[o, part], y_peers, y)

    def share_z(e, count, x_first=False):
        part = pl.ds(e, count)
        here = y if x_first else x
        from_peers((y_n if x_first else x_n)[e], lambda o: from_x.at[o, part], y_peers if x_first else x_peers, here)
        total = keep_x[here, part]
        for d in (1, 3, 2):
            total = total + from_x[(here + d) % 4, part].astype(F32)
        total = total.reshape(count, 4, 8, 256)
        for j in range(4):
            to_z[j, part] = total[:, j]
        z_n[e] = to_peers(lambda to: to_z.at[to, part], lambda o: from_z.at[o, part], line, zl)

    def share_end(e, count):
        part = pl.ds(e, count)
        from_peers(z_n[e], lambda o: from_z.at[o, part], line, zl)
        total = to_z[zl, part]
        for d in (1, 3, 2):
            total = total + from_z[(zl + d) % 4, part]
        done[part] = total

    def drain(upto):
        while drained[0] < upto:
            started[drained[0]].wait_send()
            drained[0] += 1

    drained = [0]
    x_near("own")
    site_y["own"].near()
    line_begin(0)
    x_end("own")
    site_z.near()
    site_pass("pair")
    site_y["own"].end()
    line_end(0)
    x_begin(0)
    site_y["pair"].near()
    site_z.end()
    site_pass("far")
    line_begin(1)
    x_near(0)
    site_y["pair"].end()
    x_end(0)
    site_y["far"].near()
    core_end("own")
    line_end(1)
    x_begin(1)
    line_begin(2)
    site_y["far"].end()
    core_end(0)

    make_channel(0)
    first.begin()
    first_spread(0)
    x_near(1)
    x_end(1)
    line_end(2)
    x_begin(2)
    core_end(1)
    make_channel(1)
    spread_begin(1)
    spread_end(1)
    chan_begin(2, 1)
    chan_begin(3, 1)
    x_near(2)
    first.near()
    first_spread(3)
    first_spread(1)
    x_end(2)
    core_end(2)
    make_channel(2)
    spread_begin(2)
    spread_end(2)
    chan_begin(4, 1)
    chan_begin(5, 1)
    drain(len(started) - 24)
    chan_z[2].near()
    first.end()
    first_spread(2)
    chan_z[3].near()
    fetch_left.wait()
    from_peers(left_n, left_at, y_peers, y)
    for dz in range(4):
        first_spread_end(dz)
    share_k(0, 2)
    drain(len(started) - 16)
    share_y(0, 2)
    chan_z[4].near()
    chan_z[5].near()
    chan_z[2].end()
    share_k(2, 1)
    chan_z[3].end()
    share_k(3, 1)
    share_x(0, 2)
    share_y(2, 1)
    share_x_first(3, 1)
    chan_z[4].end()
    share_k(4, 1)
    share_z(0, 2)
    share_y(4, 1)
    chan_z[5].end()
    share_k(5, 1)
    share_x(2, 1)
    share_x_first(5, 1)
    share_y_second(3, 1)
    share_x(4, 1)
    share_z(2, 1)
    share_y_second(5, 1)
    share_z(3, 1, True)
    share_z(4, 1)
    share_end(0, 2)
    share_end(2, 1)
    share_z(5, 1, True)
    drain(len(started) - 16)
    share_end(3, 1)
    share_end(4, 1)
    drain(len(started) - 3)
    share_end(5, 1)
    for s in range(2):
        result_ref[s] = jnp.concatenate([done[2 * p + s] for p in range(RUNS)], axis=0).astype(BF16)
    drain(len(started))


def local(site_tensor, left_env, right_env, mpo_out, mpo_in, mpo_ops):
    right = jnp.transpose(right_env, (1, 2, 0))
    ops = jnp.transpose(mpo_ops, (1, 2, 0)).reshape(4, 48)
    vmem = pl.BlockSpec(memory_space=pltpu.VMEM)
    hbm = pl.BlockSpec(memory_space=pl.ANY)
    result = pl.pallas_call(
        kernel,
        out_shape=jax.ShapeDtypeStruct((2, 24, 256), BF16),
        in_specs=[vmem, hbm, hbm, vmem, vmem, vmem],
        out_specs=vmem,
        scratch_shapes=[
            pltpu.VMEM((4, 4, 2, 128, 256), BF16),
            pltpu.VMEM((16, 48, 128), BF16),
            pltpu.VMEM((2, 4, RUNS, 16, 16, 128), BF16),
            pltpu.VMEM((RUNS, 2, 4, 3, 16, 16, 128), BF16),
            pltpu.VMEM((4, 4, 2, 16, 512), BF16),
            pltpu.VMEM((RUNS, 4, 2, 16, 512), BF16),
            pltpu.VMEM((2 * RUNS, 4, 4, 16, 512), BF16),
            pltpu.VMEM((4, 4, 128, 256), BF16),
            pltpu.VMEM((256, 256), F32),
            pltpu.VMEM((256, 256), BF16),
            pltpu.VMEM((4, 2 * RUNS, 128, 256), F32),
            pltpu.VMEM((2 * RUNS, 128, 256), F32),
            pltpu.VMEM((4, 2 * RUNS, 32, 256), F32),
            pltpu.VMEM((2 * RUNS, 8, 256), F32),
            pltpu.VMEM((4, 2 * RUNS, 4, 32, 256), F32),
            pltpu.VMEM((2 * RUNS, 4, 128, 256), BF16),
            pltpu.VMEM((2 * RUNS, 4, 128, 256), BF16),
            pltpu.VMEM((4, 2 * RUNS, 4, 32, 256), BF16),
            pltpu.VMEM((4, 2 * RUNS, 4, 32, 256), BF16),
            pltpu.VMEM((4, 2 * RUNS, 128, 256), BF16),
            pltpu.VMEM((4, 2 * RUNS, 128, 256), BF16),
            pltpu.VMEM((4, 2 * RUNS, 32, 256), BF16),
            pltpu.VMEM((4, 2 * RUNS, 32, 256), BF16),
            pltpu.VMEM((4, 2 * RUNS, 8, 256), F32),
            pltpu.VMEM((4, 2 * RUNS, 8, 256), F32),
            pltpu.SemaphoreType.DMA((N_COPIES,)),
            pltpu.SemaphoreType.DMA((N_COPIES,)),
            pltpu.SemaphoreType.DMA((2,)),
        ],
        compiler_params=pltpu.CompilerParams(
            collective_id=0, has_side_effects=True, vmem_limit_bytes=62 * 1024 * 1024
        ),
        cost_estimate=pl.CostEstimate(flops=3_300_000_000, bytes_accessed=2_000_000, transcendentals=0),
        name="gradient_slab",
    )(site_tensor, right, left_env, mpo_out.reshape(1, 48), mpo_in.reshape(1, 48), ops)
    return jnp.transpose(result, (2, 0, 1))


def solution(mesh):
    return jax.shard_map(
        local,
        mesh=mesh,
        in_specs=(
            P("row", None, "col"),
            P(None, "row", "col"),
            P("row", None, "col"),
            P(),
            P(),
            P(),
        ),
        out_specs=P("col", None, "row"),
        check_vma=False,
    )
```

```python
import jax
import jax.numpy as jnp
from jax import lax
from jax.experimental import pallas as pl
from jax.experimental.pallas import tpu as pltpu
from jax.sharding import PartitionSpec as P

MESH = pl.DeviceIdType.MESH
BF16 = jnp.bfloat16
F32 = jnp.float32

RUNS = 3
N_COPIES = 144


def kernel(
    site_ref, right_hbm, left_hbm, out_idx_ref, in_idx_ref, ops_ref, result_ref,
    site_all, right_in, right_own, right_line, made_first, made_all, chan_all, left, mixed, expand,
    keep_k, keep_y, keep_x, done, keep_first, to_k, from_k, to_first, from_first, to_y, from_y, to_x, from_x, to_z, from_z,
    send_sems, recv_sems, local_sems,
):
    r = lax.axis_index("row")
    c = lax.axis_index("col")
    x, zl, k = r // 8, (r // 2) % 4, r % 2
    y, zh = c // 4, c % 4

    def row_of(dx=0, dz=0, dk=0):
        return ((x + dx + 4) % 4) * 8 + ((zl + dz + 4) % 4) * 2 + (k + dk) % 2

    def col_of(dy=0, dz=0):
        return ((y + dy + 4) % 4) * 4 + (zh + dz + 4) % 4

    sibling = (row_of(dk=1), c)
    z_up, z_down = (r, col_of(dz=1)), (r, col_of(dz=-1))
    y_peers = [(r, col_of(dy=d)) for d in (1, 2, 3)]
    x_peers = [(row_of(dx=d), c) for d in (1, 2, 3)]
    line = [(row_of(dz=d), c) for d in (1, 2, 3)]
    y_up, y_down, x_up, x_down = y_peers[0], y_peers[2], x_peers[0], x_peers[2]

    barrier = pltpu.get_barrier_semaphore()
    partners = [sibling, z_up, z_down] + y_peers + x_peers + line
    for partner in partners:
        pl.semaphore_signal(barrier, inc=1, device_id=partner, device_id_type=MESH)

    fetch = pltpu.make_async_copy(right_hbm, right_in, local_sems.at[0])
    fetch.start()
    fetch_left = pltpu.make_async_copy(left_hbm.at[pl.ds(4 * y, 4)], left.at[y], local_sems.at[1])
    fetch_left.start()
    for t in range(2):
        site_all[y, 0, t] = site_ref[:, t, :]
    fetch.wait()
    by_eight = right_in[...].astype(F32).reshape(16, 6, 8, 128)
    for p in range(RUNS):
        run = jnp.concatenate([by_eight[:, p], by_eight[:, 3 + p]], axis=1).astype(BF16)
        right_own[k, x, p] = run
    pl.semaphore_wait(barrier, len(partners))

    started = []

    def send(src, dst, device):
        n = len(started)
        copy = pltpu.make_async_remote_copy(
            src_ref=src, dst_ref=dst, send_sem=send_sems.at[n], recv_sem=recv_sems.at[n],
            device_id=device, device_id_type=MESH,
        )
        copy.start()
        started.append(copy)
        return n

    def arrive(n, dst, device):
        pltpu.make_async_remote_copy(
            src_ref=dst, dst_ref=dst, send_sem=send_sems.at[n], recv_sem=recv_sems.at[n],
            device_id=device, device_id_type=MESH,
        ).wait_recv()

    def to_peers(src, dst, peers, here):
        return [send(src((here + d) % 4), dst(here), peers[d - 1]) for d in (1, 2, 3)]

    def from_peers(copies, dst, peers, here):
        for d in (1, 2, 3):
            arrive(copies[d - 1], dst((here - d + 4) % 4), peers[4 - d - 1])

    def left_at(origin):
        return left.at[origin]

    class Ring:
        def __init__(self, own, low, high, far, up, down, half, places=None):
            self.own, self.low, self.high, self.far, self.up, self.down, self.half = own, low, high, far, up, down, half
            self.places = places or (own, own, half(low, 0), half(high, 1))

        def begin(self):
            self.n_up = send(self.own, self.places[0], self.up)
            self.n_down = send(self.own, self.places[1], self.down)

        def near(self):
            arrive(self.n_up, self.low, self.down)
            self.n_low = send(self.half(self.low, 0), self.places[2], self.up)
            arrive(self.n_down, self.high, self.up)
            self.n_high = send(self.half(self.high, 1), self.places[3], self.down)

        def end(self):
            arrive(self.n_low, self.half(self.far, 0), self.down)
            arrive(self.n_high, self.half(self.far, 1), self.up)

    def first_dim(ref, i):
        return ref.at[i]

    def two_of_four(ref, i):
        return ref.at[pl.ds(2 * i, 2)]

    def half_of_v(ref, i):
        return ref.at[:, pl.ds(8 * i, 8)]

    def x_ring(at):
        return Ring(at(x), at((x + 3) % 4), at((x + 1) % 4), at((x + 2) % 4), x_up, x_down, half_of_v)

    groups = {
        "own": lambda core, origin: right_own.at[core, origin],
        0: lambda core, origin: right_line.at[0, core, origin],
        1: lambda core, origin: right_line.at[1, core, origin],
        2: lambda core, origin: right_line.at[2, core, origin],
    }
    whole = {
        "own": lambda core: right_own.at[core],
        0: lambda core: right_line.at[0, core],
        1: lambda core: right_line.at[1, core],
        2: lambda core: right_line.at[2, core],
    }
    right_x, core_n, line_n = {}, {}, {}

    def x_begin(g):
        right_x[g] = x_ring(lambda origin: groups[g](k, origin))
        right_x[g].begin()

    def x_near(g):
        right_x[g].near()

    def x_end(g):
        right_x[g].end()
        core_n[g] = send(whole[g](k), whole[g](k), sibling)

    def core_end(g):
        arrive(core_n[g], whole[g](1 - k), sibling)

    def line_begin(p):
        line_n[p] = [
            send(right_own.at[k, x, p], right_line.at[p, k, x, d - 1], line[d - 1]) for d in (1, 2, 3)
        ]

    def line_end(p):
        for d in (1, 2, 3):
            arrive(line_n[p][d - 1], right_line.at[p, k, x, d - 1], line[4 - d - 1])

    site_y = {}

    def site_pass(part):
        at = {
            "own": lambda o: site_all.at[o, 0],
            "pair": lambda o: site_all.at[o, pl.ds(1, 2)],
            "far": lambda o: site_all.at[o, 3],
        }[part]
        site_y[part] = Ring(at(y), at((y + 3) % 4), at((y + 1) % 4), at((y + 2) % 4), y_up, y_down, first_dim)
        site_y[part].begin()

    site_here = [site_all.at[y, q] for q in range(4)]
    site_z = Ring(
        site_here[0], site_here[2], site_here[1], site_here[3], z_up, z_down, first_dim,
        (site_here[2], site_here[1], site_here[3].at[0], site_here[3].at[1]),
    )
    site_z.begin()
    x_begin("own")
    site_pass("own")
    left_n = to_peers(lambda to: left_hbm.at[pl.ds(4 * to, 4)], left_at, y_peers, y)

    channel_rows = lax.broadcasted_iota(jnp.int32, (16, 48), 0)
    pick_out = channel_rows == jnp.broadcast_to(out_idx_ref[...], (16, 48))
    pick_in = (channel_rows == jnp.broadcast_to(in_idx_ref[...], (16, 48))).astype(F32).astype(BF16)
    spread = (
        lax.broadcasted_iota(jnp.int32, (128, 16), 0) // 8 == lax.broadcasted_iota(jnp.int32, (128, 16), 1)
    ).astype(F32).astype(BF16)
    same = (lax.broadcasted_iota(jnp.int32, (128, 128), 0) % 8) == (lax.broadcasted_iota(jnp.int32, (128, 128), 1) % 8)
    for s in range(2):
        for t in range(2):
            op = ops_ref[pl.ds(2 * s + t, 1), :].astype(F32)
            picked = jnp.where(pick_out, jnp.broadcast_to(op, (16, 48)), 0.0).astype(BF16)
            dense = lax.dot_general(picked, pick_in, (((1,), (1,)), ((), ())), preferred_element_type=F32).astype(BF16)
            tall = jnp.dot(spread, dense, preferred_element_type=F32).astype(BF16)
            wide = lax.dot_general(tall, spread, (((1,), (1,)), ((), ())), preferred_element_type=F32)
            expand[pl.ds(128 * s, 128), pl.ds(128 * t, 128)] = jnp.where(same, wide, 0.0).astype(BF16)

    def make_channel(p):
        def right_block(core, g, d):
            block = right_own[core, g, p] if d == 0 else right_line[p, core, g, d - 1]
            return block.reshape(256, 128)

        mixed[...] = jnp.zeros_like(mixed)

        def add_blocks(g, carry):
            update = None
            for d in range(4):
                env = jnp.concatenate([right_block(0, g, d), right_block(1, g, d)], axis=1)
                step = (zl - d - zh + 8) % 4
                site = site_all[g, step + (step // 2) * (1 - 2 * (step % 2))].reshape(256, 256)
                term = lax.dot_general(env, site, (((1,), (1,)), ((), ())), preferred_element_type=F32)
                update = term if update is None else update + term
            mixed[...] += update
            return carry

        lax.fori_loop(0, 4, add_blocks, 0)
        by_eight = mixed[...].reshape(16, 2, 8, 256)
        stacked = []
        for i in range(2):
            run = by_eight[:, i].reshape(128, 256).astype(BF16)
            stacked.append(jnp.concatenate([run[:, :128], run[:, 128:]], axis=0))
        made = jnp.dot(expand[...], jnp.concatenate(stacked, axis=1), preferred_element_type=F32)
        for s in range(2):
            for group in range(4):
                pieces = []
                for w in range(4 * group, 4 * group + 4):
                    rows = made[s * 128 + w * 8:s * 128 + w * 8 + 8, :]
                    pieces.append(jnp.concatenate([rows[:, :128], rows[:, 128:]], axis=0))
                rows = jnp.concatenate(pieces, axis=1).astype(BF16)
                if p == 0:
                    made_first[zh, group, s] = rows
                else:
                    made_all[p, group, s] = rows

    made_n = {}

    def spread_begin(p):
        run = pl.ds(2 * p, 2)
        chan_all[run, zh, y] = made_all[p, y]
        made_n[p] = to_peers(lambda to: made_all.at[p, to], lambda o: chan_all.at[run, zh, o], y_peers, y)

    def spread_end(p):
        from_peers(made_n[p], lambda o: chan_all.at[pl.ds(2 * p, 2), zh, o], y_peers, y)

    first = Ring(
        made_first.at[zh], made_first.at[(zh + 3) % 4], made_first.at[(zh + 1) % 4], made_first.at[(zh + 2) % 4],
        z_up, z_down, two_of_four,
    )
    first_n = {}

    def first_spread(dz):
        origin = (zh + dz) % 4
        chan_all[pl.ds(0, 2), origin, y] = made_first[origin, y]
        first_n[dz] = to_peers(
            lambda to: made_first.at[origin, to], lambda o: chan_all.at[pl.ds(0, 2), origin, o], y_peers, y
        )

    def first_spread_end(dz):
        origin = (zh + dz) % 4
        from_peers(first_n[dz], lambda o: chan_all.at[pl.ds(0, 2), origin, o], y_peers, y)

    chan_z = {}

    def chan_begin(e, count):
        def at(origin):
            return chan_all.at[pl.ds(e, count), origin]

        chan_z[e] = Ring(
            at(zh), at((zh + 3) % 4), at((zh + 1) % 4), at((zh + 2) % 4), z_up, z_down,
            lambda ref, i: ref.at[:, pl.ds(2 * i, 2)],
        )
        chan_z[e].begin()

    k_n, y_n, x_n, z_n = {}, {}, {}, {}

    def share_k(e, count):
        part = pl.ds(e, count)
        rows = chan_all[part].reshape(count * 256, 512)
        for j in range(4):
            total = jnp.dot(rows, left[j].reshape(512, 256), preferred_element_type=F32)
            total = total.reshape(count * 16, 2, 8, 256)
            first, second = total[:, 0].reshape(count, 128, 256), total[:, 1].reshape(count, 128, 256)
            keep_k[j, part] = jnp.where(k == 0, first, second)
            to_k[part, j] = jnp.where(k == 0, second, first).astype(BF16)
        k_n[e] = send(to_k.at[part], from_k.at[part], sibling)

    def share_y(e, count):
        part = pl.ds(e, count)
        arrive(k_n[e], from_k.at[part], sibling)
        for d in (1, 3, 2):
            to = (y + d) % 4
            to_y[to, part] = (keep_k[to, part] + from_k[part, to].astype(F32)).astype(BF16)
        y_n[e] = to_peers(lambda to: to_y.at[to, part], lambda o: from_y.at[o, part], y_peers, y)
        keep_y[part] = keep_k[y, part] + from_k[part, y].astype(F32)

    def share_x(e, count):
        part = pl.ds(e, count)
        from_peers(y_n[e], lambda o: from_y.at[o, part], y_peers, y)
        total = keep_y[part]
        for d in (1, 3, 2):
            total = total + from_y[(y + d) % 4, part].astype(F32)
        total = total.reshape(count * 4, 4, 8, 256)
        for j in range(4):
            block = total[:, j].reshape(count, 32, 256)
            keep_x[j, part] = block
            to_x[j, part] = block.astype(BF16)
        x_n[e] = to_peers(lambda to: to_x.at[to, part], lambda o: from_x.at[o, part], x_peers, x)

    def share_x_first(e, count):
        part = pl.ds(e, count)
        arrive(k_n[e], from_k.at[part], sibling)
        for j in range(4):
            total = (keep_k[j, part] + from_k[part, j].astype(F32)).reshape(count * 4, 4, 8, 256)
            for to in range(4):
                block = total[:, to].reshape(count, 32, 256)
                keep_first[to, part, j] = block
                to_first[to, part, j] = block.astype(BF16)
        x_n[e] = to_peers(lambda to: to_first.at[to, part], lambda o: from_first.at[o, part], x_peers, x)

    def share_y_second(e, count):
        part = pl.ds(e, count)
        from_peers(x_n[e], lambda o: from_first.at[o, part], x_peers, x)
        for j in range(4):
            total = keep_first[x, part, j]
            for d in (1, 3, 2):
                total = total + from_first[(x + d) % 4, part, j].astype(F32)
            keep_x[j, part] = total
            to_x[j, part] = total.astype(BF16)
        y_n[e] = to_peers(lambda to: to_x.at[to, part], lambda o: from_x.at[o, part], y_peers, y)

    def share_z(e, count, x_first=False):
        part = pl.ds(e, count)
        here = y if x_first else x
        from_peers((y_n if x_first else x_n)[e], lambda o: from_x.at[o, part], y_peers if x_first else x_peers, here)
        total = keep_x[here, part]
        for d in (1, 3, 2):
            total = total + from_x[(here + d) % 4, part].astype(F32)
        total = total.reshape(count, 4, 8, 256)
        for j in range(4):
            to_z[j, part] = total[:, j]
        z_n[e] = to_peers(lambda to: to_z.at[to, part], lambda o: from_z.at[o, part], line, zl)

    def share_end(e, count):
        part = pl.ds(e, count)
        from_peers(z_n[e], lambda o: from_z.at[o, part], line, zl)
        total = to_z[zl, part]
        for d in (1, 3, 2):
            total = total + from_z[(zl + d) % 4, part]
        done[part] = total

    def drain(upto):
        while drained[0] < upto:
            started[drained[0]].wait_send()
            drained[0] += 1

    drained = [0]
    x_near("own")
    site_y["own"].near()
    line_begin(0)
    x_end("own")
    site_z.near()
    site_pass("pair")
    site_y["own"].end()
    line_end(0)
    x_begin(0)
    site_y["pair"].near()
    site_z.end()
    site_pass("far")
    line_begin(1)
    x_near(0)
    site_y["pair"].end()
    x_end(0)
    site_y["far"].near()
    core_end("own")
    line_end(1)
    x_begin(1)
    line_begin(2)
    site_y["far"].end()
    core_end(0)

    make_channel(0)
    first.begin()
    first_spread(0)
    x_near(1)
    x_end(1)
    line_end(2)
    x_begin(2)
    core_end(1)
    make_channel(1)
    spread_begin(1)
    spread_end(1)
    chan_begin(2, 1)
    x_near(2)
    first.near()
    chan_begin(3, 1)
    first_spread(3)
    first_spread(1)
    x_end(2)
    core_end(2)
    make_channel(2)
    spread_begin(2)
    spread_end(2)
    chan_begin(4, 1)
    drain(len(started) - 24)
    chan_z[2].near()
    chan_begin(5, 1)
    first.end()
    first_spread(2)
    chan_z[3].near()
    fetch_left.wait()
    from_peers(left_n, left_at, y_peers, y)
    for dz in range(4):
        first_spread_end(dz)
    share_k(0, 2)
    drain(len(started) - 16)
    share_y(0, 2)
    chan_z[4].near()
    chan_z[5].near()
    chan_z[2].end()
    share_k(2, 1)
    chan_z[3].end()
    share_k(3, 1)
    share_x(0, 2)
    share_y(2, 1)
    share_x_first(3, 1)
    chan_z[4].end()
    share_k(4, 1)
    share_y(4, 1)
    chan_z[5].end()
    share_k(5, 1)
    share_x(2, 1)
    share_x_first(5, 1)
    share_z(0, 2)
    share_y_second(3, 1)
    share_x(4, 1)
    share_z(2, 1)
    share_y_second(5, 1)
    share_z(3, 1, True)
    share_z(4, 1)
    share_end(0, 2)
    share_end(2, 1)
    share_z(5, 1, True)
    drain(len(started) - 16)
    share_end(3, 1)
    share_end(4, 1)
    drain(len(started) - 3)
    share_end(5, 1)
    for s in range(2):
        result_ref[s] = jnp.concatenate([done[2 * p + s] for p in range(RUNS)], axis=0).astype(BF16)
    drain(len(started))


def local(site_tensor, left_env, right_env, mpo_out, mpo_in, mpo_ops):
    right = jnp.transpose(right_env, (1, 2, 0))
    ops = jnp.transpose(mpo_ops, (1, 2, 0)).reshape(4, 48)
    vmem = pl.BlockSpec(memory_space=pltpu.VMEM)
    hbm = pl.BlockSpec(memory_space=pl.ANY)
    result = pl.pallas_call(
        kernel,
        out_shape=jax.ShapeDtypeStruct((2, 24, 256), BF16),
        in_specs=[vmem, hbm, hbm, vmem, vmem, vmem],
        out_specs=vmem,
        scratch_shapes=[
            pltpu.VMEM((4, 4, 2, 128, 256), BF16),
            pltpu.VMEM((16, 48, 128), BF16),
            pltpu.VMEM((2, 4, RUNS, 16, 16, 128), BF16),
            pltpu.VMEM((RUNS, 2, 4, 3, 16, 16, 128), BF16),
            pltpu.VMEM((4, 4, 2, 16, 512), BF16),
            pltpu.VMEM((RUNS, 4, 2, 16, 512), BF16),
            pltpu.VMEM((2 * RUNS, 4, 4, 16, 512), BF16),
            pltpu.VMEM((4, 4, 128, 256), BF16),
            pltpu.VMEM((256, 256), F32),
            pltpu.VMEM((256, 256), BF16),
            pltpu.VMEM((4, 2 * RUNS, 128, 256), F32),
            pltpu.VMEM((2 * RUNS, 128, 256), F32),
            pltpu.VMEM((4, 2 * RUNS, 32, 256), F32),
            pltpu.VMEM((2 * RUNS, 8, 256), F32),
            pltpu.VMEM((4, 2 * RUNS, 4, 32, 256), F32),
            pltpu.VMEM((2 * RUNS, 4, 128, 256), BF16),
            pltpu.VMEM((2 * RUNS, 4, 128, 256), BF16),
            pltpu.VMEM((4, 2 * RUNS, 4, 32, 256), BF16),
            pltpu.VMEM((4, 2 * RUNS, 4, 32, 256), BF16),
            pltpu.VMEM((4, 2 * RUNS, 128, 256), BF16),
            pltpu.VMEM((4, 2 * RUNS, 128, 256), BF16),
            pltpu.VMEM((4, 2 * RUNS, 32, 256), BF16),
            pltpu.VMEM((4, 2 * RUNS, 32, 256), BF16),
            pltpu.VMEM((4, 2 * RUNS, 8, 256), F32),
            pltpu.VMEM((4, 2 * RUNS, 8, 256), F32),
            pltpu.SemaphoreType.DMA((N_COPIES,)),
            pltpu.SemaphoreType.DMA((N_COPIES,)),
            pltpu.SemaphoreType.DMA((2,)),
        ],
        compiler_params=pltpu.CompilerParams(
            collective_id=0, has_side_effects=True, vmem_limit_bytes=62 * 1024 * 1024
        ),
        cost_estimate=pl.CostEstimate(flops=3_300_000_000, bytes_accessed=2_000_000, transcendentals=0),
        name="gradient_slab",
    )(site_tensor, right, left_env, mpo_out.reshape(1, 48), mpo_in.reshape(1, 48), ops)
    return jnp.transpose(result, (2, 0, 1))


def solution(mesh):
    return jax.shard_map(
        local,
        mesh=mesh,
        in_specs=(
            P("row", None, "col"),
            P(None, "row", "col"),
            P("row", None, "col"),
            P(),
            P(),
            P(),
        ),
        out_specs=P("col", None, "row"),
        check_vma=False,
    )
```

```python
import jax
import jax.numpy as jnp
from jax import lax
from jax.experimental import pallas as pl
from jax.experimental.pallas import tpu as pltpu
from jax.sharding import PartitionSpec as P

MESH = pl.DeviceIdType.MESH
BF16 = jnp.bfloat16
F32 = jnp.float32

RUNS = 3
N_COPIES = 144


def kernel(
    site_ref, right_hbm, left_hbm, out_idx_ref, in_idx_ref, ops_ref, result_ref,
    site_all, right_in, right_own, right_line, made_first, made_all, chan_all, left, mixed, expand,
    keep_k, keep_y, keep_x, done, keep_first, to_k, from_k, to_first, from_first, to_y, from_y, to_x, from_x, to_z, from_z,
    send_sems, recv_sems, local_sems,
):
    r = lax.axis_index("row")
    c = lax.axis_index("col")
    x, zl, k = r // 8, (r // 2) % 4, r % 2
    y, zh = c // 4, c % 4

    def row_of(dx=0, dz=0, dk=0):
        return ((x + dx + 4) % 4) * 8 + ((zl + dz + 4) % 4) * 2 + (k + dk) % 2

    def col_of(dy=0, dz=0):
        return ((y + dy + 4) % 4) * 4 + (zh + dz + 4) % 4

    sibling = (row_of(dk=1), c)
    z_up, z_down = (r, col_of(dz=1)), (r, col_of(dz=-1))
    y_peers = [(r, col_of(dy=d)) for d in (1, 2, 3)]
    x_peers = [(row_of(dx=d), c) for d in (1, 2, 3)]
    line = [(row_of(dz=d), c) for d in (1, 2, 3)]
    y_up, y_down, x_up, x_down = y_peers[0], y_peers[2], x_peers[0], x_peers[2]

    barrier = pltpu.get_barrier_semaphore()
    partners = [sibling, z_up, z_down] + y_peers + x_peers + line
    for partner in partners:
        pl.semaphore_signal(barrier, inc=1, device_id=partner, device_id_type=MESH)

    fetch = pltpu.make_async_copy(right_hbm, right_in, local_sems.at[0])
    fetch.start()
    fetch_left = pltpu.make_async_copy(left_hbm.at[pl.ds(4 * y, 4)], left.at[y], local_sems.at[1])
    fetch_left.start()
    for t in range(2):
        site_all[y, 0, t] = site_ref[:, t, :]
    fetch.wait()
    by_eight = right_in[...].astype(F32).reshape(16, 6, 8, 128)
    for p in range(RUNS):
        run = jnp.concatenate([by_eight[:, p], by_eight[:, 3 + p]], axis=1).astype(BF16)
        right_own[k, x, p] = run
    pl.semaphore_wait(barrier, len(partners))

    started = []

    def send(src, dst, device):
        n = len(started)
        copy = pltpu.make_async_remote_copy(
            src_ref=src, dst_ref=dst, send_sem=send_sems.at[n], recv_sem=recv_sems.at[n],
            device_id=device, device_id_type=MESH,
        )
        copy.start()
        started.append(copy)
        return n

    def arrive(n, dst, device):
        pltpu.make_async_remote_copy(
            src_ref=dst, dst_ref=dst, send_sem=send_sems.at[n], recv_sem=recv_sems.at[n],
            device_id=device, device_id_type=MESH,
        ).wait_recv()

    def to_peers(src, dst, peers, here):
        return [send(src((here + d) % 4), dst(here), peers[d - 1]) for d in (1, 2, 3)]

    def from_peers(copies, dst, peers, here):
        for d in (1, 2, 3):
            arrive(copies[d - 1], dst((here - d + 4) % 4), peers[4 - d - 1])

    def left_at(origin):
        return left.at[origin]

    class Ring:
        def __init__(self, own, low, high, far, up, down, half, places=None):
            self.own, self.low, self.high, self.far, self.up, self.down, self.half = own, low, high, far, up, down, half
            self.places = places or (own, own, half(low, 0), half(high, 1))

        def begin(self):
            self.n_up = send(self.own, self.places[0], self.up)
            self.n_down = send(self.own, self.places[1], self.down)

        def near(self):
            arrive(self.n_up, self.low, self.down)
            self.n_low = send(self.half(self.low, 0), self.places[2], self.up)
            arrive(self.n_down, self.high, self.up)
            self.n_high = send(self.half(self.high, 1), self.places[3], self.down)

        def end(self):
            arrive(self.n_low, self.half(self.far, 0), self.down)
            arrive(self.n_high, self.half(self.far, 1), self.up)

    def first_dim(ref, i):
        return ref.at[i]

    def two_of_four(ref, i):
        return ref.at[pl.ds(2 * i, 2)]

    def half_of_v(ref, i):
        return ref.at[:, pl.ds(8 * i, 8)]

    def x_ring(at):
        return Ring(at(x), at((x + 3) % 4), at((x + 1) % 4), at((x + 2) % 4), x_up, x_down, half_of_v)

    groups = {
        "own": lambda core, origin: right_own.at[core, origin],
        0: lambda core, origin: right_line.at[0, core, origin],
        1: lambda core, origin: right_line.at[1, core, origin],
        2: lambda core, origin: right_line.at[2, core, origin],
    }
    whole = {
        "own": lambda core: right_own.at[core],
        0: lambda core: right_line.at[0, core],
        1: lambda core: right_line.at[1, core],
        2: lambda core: right_line.at[2, core],
    }
    right_x, core_n, line_n = {}, {}, {}

    def x_begin(g):
        right_x[g] = x_ring(lambda origin: groups[g](k, origin))
        right_x[g].begin()

    def x_near(g):
        right_x[g].near()

    def x_end(g):
        right_x[g].end()
        core_n[g] = send(whole[g](k), whole[g](k), sibling)

    def core_end(g):
        arrive(core_n[g], whole[g](1 - k), sibling)

    def line_begin(p):
        line_n[p] = [
            send(right_own.at[k, x, p], right_line.at[p, k, x, d - 1], line[d - 1]) for d in (1, 2, 3)
        ]

    def line_end(p):
        for d in (1, 2, 3):
            arrive(line_n[p][d - 1], right_line.at[p, k, x, d - 1], line[4 - d - 1])

    site_y = {}

    def site_pass(part):
        at = {
            "own": lambda o: site_all.at[o, 0],
            "pair": lambda o: site_all.at[o, pl.ds(1, 2)],
            "far": lambda o: site_all.at[o, 3],
        }[part]
        site_y[part] = Ring(at(y), at((y + 3) % 4), at((y + 1) % 4), at((y + 2) % 4), y_up, y_down, first_dim)
        site_y[part].begin()

    site_here = [site_all.at[y, q] for q in range(4)]
    site_z = Ring(
        site_here[0], site_here[2], site_here[1], site_here[3], z_up, z_down, first_dim,
        (site_here[2], site_here[1], site_here[3].at[0], site_here[3].at[1]),
    )
    site_z.begin()
    x_begin("own")
    site_pass("own")
    left_n = to_peers(lambda to: left_hbm.at[pl.ds(4 * to, 4)], left_at, y_peers, y)

    channel_rows = lax.broadcasted_iota(jnp.int32, (16, 48), 0)
    pick_out = channel_rows == jnp.broadcast_to(out_idx_ref[...], (16, 48))
    pick_in = (channel_rows == jnp.broadcast_to(in_idx_ref[...], (16, 48))).astype(F32).astype(BF16)
    spread = (
        lax.broadcasted_iota(jnp.int32, (128, 16), 0) // 8 == lax.broadcasted_iota(jnp.int32, (128, 16), 1)
    ).astype(F32).astype(BF16)
    same = (lax.broadcasted_iota(jnp.int32, (128, 128), 0) % 8) == (lax.broadcasted_iota(jnp.int32, (128, 128), 1) % 8)
    for s in range(2):
        for t in range(2):
            op = ops_ref[pl.ds(2 * s + t, 1), :].astype(F32)
            picked = jnp.where(pick_out, jnp.broadcast_to(op, (16, 48)), 0.0).astype(BF16)
            dense = lax.dot_general(picked, pick_in, (((1,), (1,)), ((), ())), preferred_element_type=F32).astype(BF16)
            tall = jnp.dot(spread, dense, preferred_element_type=F32).astype(BF16)
            wide = lax.dot_general(tall, spread, (((1,), (1,)), ((), ())), preferred_element_type=F32)
            expand[pl.ds(128 * s, 128), pl.ds(128 * t, 128)] = jnp.where(same, wide, 0.0).astype(BF16)

    def make_channel(p):
        def right_block(core, g, d):
            block = right_own[core, g, p] if d == 0 else right_line[p, core, g, d - 1]
            return block.reshape(256, 128)

        mixed[...] = jnp.zeros_like(mixed)

        def add_blocks(g, carry):
            update = None
            for d in range(4):
                env = jnp.concatenate([right_block(0, g, d), right_block(1, g, d)], axis=1)
                step = (zl - d - zh + 8) % 4
                site = site_all[g, step + (step // 2) * (1 - 2 * (step % 2))].reshape(256, 256)
                term = lax.dot_general(env, site, (((1,), (1,)), ((), ())), preferred_element_type=F32)
                update = term if update is None else update + term
            mixed[...] += update
            return carry

        lax.fori_loop(0, 4, add_blocks, 0)
        by_eight = mixed[...].reshape(16, 2, 8, 256)
        stacked = []
        for i in range(2):
            run = by_eight[:, i].reshape(128, 256).astype(BF16)
            stacked.append(jnp.concatenate([run[:, :128], run[:, 128:]], axis=0))
        made = jnp.dot(expand[...], jnp.concatenate(stacked, axis=1), preferred_element_type=F32)
        for s in range(2):
            for group in range(4):
                pieces = []
                for w in range(4 * group, 4 * group + 4):
                    rows = made[s * 128 + w * 8:s * 128 + w * 8 + 8, :]
                    pieces.append(jnp.concatenate([rows[:, :128], rows[:, 128:]], axis=0))
                rows = jnp.concatenate(pieces, axis=1).astype(BF16)
                if p == 0:
                    made_first[zh, group, s] = rows
                else:
                    made_all[p, group, s] = rows

    made_n = {}

    def spread_begin(p):
        run = pl.ds(2 * p, 2)
        chan_all[run, zh, y] = made_all[p, y]
        made_n[p] = to_peers(lambda to: made_all.at[p, to], lambda o: chan_all.at[run, zh, o], y_peers, y)

    def spread_end(p):
        from_peers(made_n[p], lambda o: chan_all.at[pl.ds(2 * p, 2), zh, o], y_peers, y)

    first = Ring(
        made_first.at[zh], made_first.at[(zh + 3) % 4], made_first.at[(zh + 1) % 4], made_first.at[(zh + 2) % 4],
        z_up, z_down, two_of_four,
    )
    first_n = {}

    def first_spread(dz):
        origin = (zh + dz) % 4
        chan_all[pl.ds(0, 2), origin, y] = made_first[origin, y]
        first_n[dz] = to_peers(
            lambda to: made_first.at[origin, to], lambda o: chan_all.at[pl.ds(0, 2), origin, o], y_peers, y
        )

    def first_spread_end(dz):
        origin = (zh + dz) % 4
        from_peers(first_n[dz], lambda o: chan_all.at[pl.ds(0, 2), origin, o], y_peers, y)

    chan_z = {}

    def chan_begin(e, count):
        def at(origin):
            return chan_all.at[pl.ds(e, count), origin]

        chan_z[e] = Ring(
            at(zh), at((zh + 3) % 4), at((zh + 1) % 4), at((zh + 2) % 4), z_up, z_down,
            lambda ref, i: ref.at[:, pl.ds(2 * i, 2)],
        )
        chan_z[e].begin()

    k_n, y_n, x_n, z_n = {}, {}, {}, {}

    def share_k(e, count):
        part = pl.ds(e, count)
        rows = chan_all[part].reshape(count * 256, 512)
        for j in range(4):
            total = jnp.dot(rows, left[j].reshape(512, 256), preferred_element_type=F32)
            total = total.reshape(count * 16, 2, 8, 256)
            first, second = total[:, 0].reshape(count, 128, 256), total[:, 1].reshape(count, 128, 256)
            keep_k[j, part] = jnp.where(k == 0, first, second)
            to_k[part, j] = jnp.where(k == 0, second, first).astype(BF16)
        k_n[e] = send(to_k.at[part], from_k.at[part], sibling)

    def share_y(e, count):
        part = pl.ds(e, count)
        arrive(k_n[e], from_k.at[part], sibling)
        for d in (1, 3, 2):
            to = (y + d) % 4
            to_y[to, part] = (keep_k[to, part] + from_k[part, to].astype(F32)).astype(BF16)
        y_n[e] = to_peers(lambda to: to_y.at[to, part], lambda o: from_y.at[o, part], y_peers, y)
        keep_y[part] = keep_k[y, part] + from_k[part, y].astype(F32)

    def share_x(e, count):
        part = pl.ds(e, count)
        from_peers(y_n[e], lambda o: from_y.at[o, part], y_peers, y)
        total = keep_y[part]
        for d in (1, 3, 2):
            total = total + from_y[(y + d) % 4, part].astype(F32)
        total = total.reshape(count * 4, 4, 8, 256)
        for j in range(4):
            block = total[:, j].reshape(count, 32, 256)
            keep_x[j, part] = block
            to_x[j, part] = block.astype(BF16)
        x_n[e] = to_peers(lambda to: to_x.at[to, part], lambda o: from_x.at[o, part], x_peers, x)

    def share_x_first(e, count):
        part = pl.ds(e, count)
        arrive(k_n[e], from_k.at[part], sibling)
        for j in range(4):
            total = (keep_k[j, part] + from_k[part, j].astype(F32)).reshape(count * 4, 4, 8, 256)
            for to in range(4):
                block = total[:, to].reshape(count, 32, 256)
                keep_first[to, part, j] = block
                to_first[to, part, j] = block.astype(BF16)
        x_n[e] = to_peers(lambda to: to_first.at[to, part], lambda o: from_first.at[o, part], x_peers, x)

    def share_y_second(e, count):
        part = pl.ds(e, count)
        from_peers(x_n[e], lambda o: from_first.at[o, part], x_peers, x)
        for j in range(4):
            total = keep_first[x, part, j]
            for d in (1, 3, 2):
                total = total + from_first[(x + d) % 4, part, j].astype(F32)
            keep_x[j, part] = total
            to_x[j, part] = total.astype(BF16)
        y_n[e] = to_peers(lambda to: to_x.at[to, part], lambda o: from_x.at[o, part], y_peers, y)

    def share_z(e, count, x_first=False):
        part = pl.ds(e, count)
        here = y if x_first else x
        from_peers((y_n if x_first else x_n)[e], lambda o: from_x.at[o, part], y_peers if x_first else x_peers, here)
        total = keep_x[here, part]
        for d in (1, 3, 2):
            total = total + from_x[(here + d) % 4, part].astype(F32)
        total = total.reshape(count, 4, 8, 256)
        for j in range(4):
            to_z[j, part] = total[:, j]
        z_n[e] = to_peers(lambda to: to_z.at[to, part], lambda o: from_z.at[o, part], line, zl)

    def share_end(e, count):
        part = pl.ds(e, count)
        from_peers(z_n[e], lambda o: from_z.at[o, part], line, zl)
        total = to_z[zl, part]
        for d in (1, 3, 2):
            total = total + from_z[(zl + d) % 4, part]
        done[part] = total

    def drain(upto):
        while drained[0] < upto:
            started[drained[0]].wait_send()
            drained[0] += 1

    drained = [0]
    x_near("own")
    site_y["own"].near()
    line_begin(0)
    x_end("own")
    site_z.near()
    site_pass("pair")
    site_y["own"].end()
    line_end(0)
    x_begin(0)
    site_y["pair"].near()
    site_z.end()
    site_pass("far")
    line_begin(1)
    x_near(0)
    site_y["pair"].end()
    x_end(0)
    site_y["far"].near()
    core_end("own")
    line_end(1)
    x_begin(1)
    line_begin(2)
    site_y["far"].end()
    core_end(0)

    make_channel(0)
    first.begin()
    first_spread(0)
    x_near(1)
    x_end(1)
    line_end(2)
    x_begin(2)
    core_end(1)
    make_channel(1)
    spread_begin(1)
    spread_end(1)
    chan_begin(2, 1)
    x_near(2)
    first.near()
    chan_begin(3, 1)
    first_spread(3)
    first_spread(1)
    x_end(2)
    core_end(2)
    make_channel(2)
    spread_begin(2)
    spread_end(2)
    chan_begin(4, 1)
    drain(len(started) - 24)
    chan_z[2].near()
    chan_z[3].near()
    chan_begin(5, 1)
    first.end()
    first_spread(2)
    fetch_left.wait()
    from_peers(left_n, left_at, y_peers, y)
    for dz in range(4):
        first_spread_end(dz)
    share_k(0, 2)
    drain(len(started) - 16)
    share_y(0, 2)
    chan_z[4].near()
    chan_z[5].near()
    chan_z[2].end()
    share_k(2, 1)
    chan_z[3].end()
    share_k(3, 1)
    share_x(0, 2)
    share_y(2, 1)
    share_x_first(3, 1)
    chan_z[4].end()
    share_k(4, 1)
    share_y(4, 1)
    chan_z[5].end()
    share_k(5, 1)
    share_x(2, 1)
    share_x_first(5, 1)
    share_z(0, 2)
    share_y_second(3, 1)
    share_x(4, 1)
    share_z(2, 1)
    share_y_second(5, 1)
    share_z(3, 1, True)
    share_z(4, 1)
    share_end(0, 2)
    share_end(2, 1)
    share_z(5, 1, True)
    drain(len(started) - 16)
    share_end(3, 1)
    share_end(4, 1)
    drain(len(started) - 3)
    share_end(5, 1)
    for s in range(2):
        result_ref[s] = jnp.concatenate([done[2 * p + s] for p in range(RUNS)], axis=0).astype(BF16)
    drain(len(started))


def local(site_tensor, left_env, right_env, mpo_out, mpo_in, mpo_ops):
    right = jnp.transpose(right_env, (1, 2, 0))
    ops = jnp.transpose(mpo_ops, (1, 2, 0)).reshape(4, 48)
    vmem = pl.BlockSpec(memory_space=pltpu.VMEM)
    hbm = pl.BlockSpec(memory_space=pl.ANY)
    result = pl.pallas_call(
        kernel,
        out_shape=jax.ShapeDtypeStruct((2, 24, 256), BF16),
        in_specs=[vmem, hbm, hbm, vmem, vmem, vmem],
        out_specs=vmem,
        scratch_shapes=[
            pltpu.VMEM((4, 4, 2, 128, 256), BF16),
            pltpu.VMEM((16, 48, 128), BF16),
            pltpu.VMEM((2, 4, RUNS, 16, 16, 128), BF16),
            pltpu.VMEM((RUNS, 2, 4, 3, 16, 16, 128), BF16),
            pltpu.VMEM((4, 4, 2, 16, 512), BF16),
            pltpu.VMEM((RUNS, 4, 2, 16, 512), BF16),
            pltpu.VMEM((2 * RUNS, 4, 4, 16, 512), BF16),
            pltpu.VMEM((4, 4, 128, 256), BF16),
            pltpu.VMEM((256, 256), F32),
            pltpu.VMEM((256, 256), BF16),
            pltpu.VMEM((4, 2 * RUNS, 128, 256), F32),
            pltpu.VMEM((2 * RUNS, 128, 256), F32),
            pltpu.VMEM((4, 2 * RUNS, 32, 256), F32),
            pltpu.VMEM((2 * RUNS, 8, 256), F32),
            pltpu.VMEM((4, 2 * RUNS, 4, 32, 256), F32),
            pltpu.VMEM((2 * RUNS, 4, 128, 256), BF16),
            pltpu.VMEM((2 * RUNS, 4, 128, 256), BF16),
            pltpu.VMEM((4, 2 * RUNS, 4, 32, 256), BF16),
            pltpu.VMEM((4, 2 * RUNS, 4, 32, 256), BF16),
            pltpu.VMEM((4, 2 * RUNS, 128, 256), BF16),
            pltpu.VMEM((4, 2 * RUNS, 128, 256), BF16),
            pltpu.VMEM((4, 2 * RUNS, 32, 256), BF16),
            pltpu.VMEM((4, 2 * RUNS, 32, 256), BF16),
            pltpu.VMEM((4, 2 * RUNS, 8, 256), F32),
            pltpu.VMEM((4, 2 * RUNS, 8, 256), F32),
            pltpu.SemaphoreType.DMA((N_COPIES,)),
            pltpu.SemaphoreType.DMA((N_COPIES,)),
            pltpu.SemaphoreType.DMA((2,)),
        ],
        compiler_params=pltpu.CompilerParams(
            collective_id=0, has_side_effects=True, vmem_limit_bytes=62 * 1024 * 1024
        ),
        cost_estimate=pl.CostEstimate(flops=3_300_000_000, bytes_accessed=2_000_000, transcendentals=0),
        name="gradient_slab",
    )(site_tensor, right, left_env, mpo_out.reshape(1, 48), mpo_in.reshape(1, 48), ops)
    return jnp.transpose(result, (2, 0, 1))


def solution(mesh):
    return jax.shard_map(
        local,
        mesh=mesh,
        in_specs=(
            P("row", None, "col"),
            P(None, "row", "col"),
            P("row", None, "col"),
            P(),
            P(),
            P(),
        ),
        out_specs=P("col", None, "row"),
        check_vma=False,
    )
```
